256 devices in a mesh: gx: 16 (over y, x), gy: 16 (over z, core).
Axes of the slice: x: 4, y: 4, z: 8, core: 2. Of those that a mesh axis runs over, the one named last changes fastest.
Arguments:
- coords: float32 [3, 1048576], P(None, ('gx', 'gy')), may hold values from 0 to 8
- noise: float32 [1048576], P(('gx', 'gy')), may hold values from 0.5 to 2
- order: int32 [16, 65536], P('gx', 'gy'), may hold values from 0 to 65535, as said below
- probes: bfloat16 [64, 1048576], P(None, ('gx', 'gy')), may hold values from -5 to 5
- factors: bfloat16 [10, 2, 32, 1048576], P(None, None, None, ('gx', 'gy')), may hold values from -1 to 1
Outputs:
- product: float32 [64, 1048576], P(None, ('gx', 'gy'))
The draws below stay inside these ranges and needn't reach their ends.
Inputs may be any that keep to these rules, and one draw needn't show every extreme that they name: Each row of order lists every number from 0 to 65535 once; every run of 4096 tree positions starting at a multiple of 4096 takes exactly 256 numbers from each run of 4096 input indices starting at a multiple of 4096.
All inputs are finite; a program needn't handle non-finite values.
Results may differ from the reference program's by a relative error of at most 0.0029.
Values may be sent and summed in bfloat16 or wider, within the bound.
A program may use at most 128 MiB of HBM per device.

```python
import math
import jax
import jax.numpy as jnp
from jax import lax

LEAF = 1024
RANK = 32
PROBES = 64
PTS_DEV = 4096
NPTS = 1048576
GROUP = 65536
LEVELS = 10


def draw_factors(key, part):
    key = jax.random.fold_in(key, 7)
    layers = []
    for tier_index in range(LEVELS):
        tier_key = jax.random.fold_in(key, tier_index)
        scale = (0.5 / (RANK * LEAF * 2.0 ** tier_index) ** 0.5) ** 0.5
        base = jax.random.normal(tier_key, (2, RANK, NPTS), jnp.float32)
        layers.append((base * scale).astype(jnp.bfloat16))
    return jnp.stack(layers)


def draw_order(key, part):
    key = jax.random.fold_in(key, 11)
    groups = NPTS // GROUP
    inner = GROUP // PTS_DEV
    slot_size = PTS_DEV // inner
    owner_keys = jax.random.split(jax.random.fold_in(key, 1), groups * inner)
    owner_perms = jax.vmap(lambda one_key: jax.random.permutation(one_key, PTS_DEV))(owner_keys)
    owner_perms = owner_perms.astype(jnp.int32).reshape(groups, inner, inner, slot_size)
    owner_base = (jnp.arange(inner, dtype=jnp.int32) * PTS_DEV)[None, :, None, None]
    picked = (owner_perms + owner_base).transpose(0, 2, 1, 3).reshape(groups * inner, PTS_DEV)
    place_keys = jax.random.split(jax.random.fold_in(key, 2), groups * inner)
    places = jax.vmap(lambda one_key: jax.random.permutation(one_key, PTS_DEV))(place_keys).astype(jnp.int32)
    shuffled = jnp.take_along_axis(picked, places, axis=1)
    return shuffled.reshape(groups, GROUP)


def block_levels(own_key, extent, pieces, least, largest):
    loudness = 1.0
    for axis_at, blocks in pieces:
        heights = jax.random.uniform(jax.random.fold_in(jax.random.fold_in(own_key, 6), axis_at), (blocks,), jnp.float32, least / len(pieces), largest / len(pieces))
        loudness = loudness * jnp.repeat(jnp.exp(heights), extent[axis_at] // blocks).reshape((-1,) + (1,) * (len(extent) - 1 - axis_at))
    return loudness


def bell_draw(rng, shape, deviation, reach, pieces=(), held_as=jnp.bfloat16):
    values = jax.random.normal(rng, shape, jnp.float32) * deviation
    if len(pieces) > 0:
        values = block_levels(rng, shape, pieces, -0.22, 0.18) * values
    return jnp.clip(values, min=-reach, max=reach).astype(held_as)


def setup_inputs(seed: int = 0) -> dict:
    key_of = jax.random.split(jax.random.key(seed), 6)
    coords = jnp.clip(8.0 * jax.random.uniform(key_of[0], (3, NPTS), jnp.float32) ** block_levels(key_of[0], (3, NPTS), ((1, 256),), -0.2, 0.2), 0.0, 8.0)
    noise = jnp.clip(jnp.exp(math.log(2.0) - 1.3862944 * jax.random.uniform(key_of[1], (NPTS,), jnp.float32) ** block_levels(key_of[1], (NPTS,), ((0, 256),), -0.2, 0.2)), 0.5, 2.0)
    order = draw_order(jax.random.fold_in(key_of[5], 71), 0)
    probes = bell_draw(key_of[3], (PROBES, NPTS), 1.0, 5.0, ((1, 256),))
    factors = draw_factors(jax.random.fold_in(key_of[5], 71), 0)
    return dict(coords=coords, noise=noise, order=order, probes=probes, factors=factors)


SQRT_THREE = 1.7320508075688772

def leaf_kernel(spots, spread):
    square = (spots[0][:, None] - spots[0][None, :]) ** 2
    square = square + (spots[1][:, None] - spots[1][None, :]) ** 2
    square = square + (spots[2][:, None] - spots[2][None, :]) ** 2
    scaled = jnp.sqrt(square) * SQRT_THREE
    return ((1.0 + scaled) * jnp.exp(-scaled) + jnp.diag(spread)).astype(jnp.bfloat16)

def level_term(pair, probes, width):
    total = probes.shape[1]
    nodes = total // width
    right = pair[1].astype(jnp.float32).reshape(RANK, nodes, width)
    left = pair[0].astype(jnp.float32).reshape(RANK, nodes, width)
    vectors = probes.astype(jnp.float32).reshape(PROBES, nodes, width)
    coeff = jnp.einsum('rkn,pkn->krp', right, vectors)
    sibling = coeff.reshape(nodes // 2, 2, RANK, PROBES)[:, ::-1].reshape(nodes, RANK, PROBES).astype(jnp.bfloat16)
    return jnp.einsum('rkn,krp->pkn', left, sibling.astype(jnp.float32)).reshape(PROBES, total)

def reference(coords, noise, order, probes, factors):
    groups = order.shape[0]
    group_size = order.shape[1]
    grouped = coords.reshape(3, groups, group_size)
    tree_coords = jnp.take_along_axis(grouped, order[None, :, :], axis=2).reshape(3, NPTS)
    tree_noise = jnp.take_along_axis(noise.reshape(groups, group_size), order, axis=1).reshape(NPTS)
    leaves = NPTS // LEAF
    leaf_coords = tree_coords.reshape(3, leaves, LEAF).transpose(1, 0, 2)
    leaf_noise = tree_noise.reshape(leaves, LEAF)
    leaf_probes = probes.reshape(PROBES, leaves, LEAF).transpose(1, 0, 2)

    def one_leaf(items):
        spots, spread, vectors = items
        return jnp.dot(vectors, leaf_kernel(spots, spread), preferred_element_type=jnp.float32)
    dense = lax.map(one_leaf, (leaf_coords, leaf_noise, leaf_probes))
    product = dense.transpose(1, 0, 2).reshape(PROBES, NPTS)
    for tier_index in range(LEVELS):
        product = product + level_term(factors[tier_index], probes, LEAF * 2 ** tier_index)
    return product
```

```python
import functools

import jax
import jax.numpy as jnp
from jax import lax
from jax.experimental import pallas as pl
from jax.experimental.pallas import tpu as pltpu
from jax.sharding import PartitionSpec as P

LEAF = 1024
RANK = 32
PROBES = 64
LANES = 128
TILE = 256
NT = (((1,), (1,)), ((), ()))
TN = (((0,), (0,)), ((), ()))
SQRT_THREE = 1.7320508075688772


def dot(a, b, dims=(((1,), (0,)), ((), ()))):
    return lax.dot_general(a, b, dims, preferred_element_type=jnp.float32)


def look_up(table, first, second):
    shape = (8, LANES)
    found = []
    for picks in (first, second):
        picks = jnp.broadcast_to(picks, shape)
        lane = picks & (LANES - 1)
        upper = picks >> 8
        out = jnp.zeros(shape, jnp.float32)
        for r, vector in enumerate(table):
            out = jnp.where(
                upper == r,
                jnp.take_along_axis(vector, lane, axis=1, mode="promise_in_bounds"),
                out,
            )
        found.append((out, ((picks >> 7) & 1) == 0))
    row = lax.broadcasted_iota(jnp.int32, shape, 0)
    (one, one_low), (two, two_low) = found
    return jnp.where(
        row < 4,
        jnp.where(one_low, one, pltpu.roll(one, 4, 0)),
        jnp.where(two_low, pltpu.roll(two, 4, 0), two),
    )


def exchange_kernel(
    inner,
    outer,
    coords_hbm,
    noise_hbm,
    order_hbm,
    probes_hbm,
    factors_hbm,
    tree_ref,
    sib_ref,
    near_ref,
    coords,
    noise,
    order,
    probes,
    right,
    counts,
    slots,
    table,
    ask,
    asked,
    give,
    given,
    part,
    parts,
    inner_sib,
    total,
    totals,
    pairs,
    back,
    backs,
    load_sem,
    send_sem,
    recv_sem,
):
    gx, gy = lax.axis_index("gx"), lax.axis_index("gy")
    points = order.shape[1]
    slot = points // inner
    levels = right.shape[0]
    far = levels - 2
    inner_bits = inner.bit_length() - 1
    outer_bits = outer.bit_length() - 1
    share = PROBES // inner

    barrier = pltpu.get_barrier_semaphore()
    for axis, own, size in (("gy", gy, inner), ("gx", gx, outer)):

        @pl.loop(1, size)
        def _(j):
            pl.semaphore_signal(barrier, inc=1, device_id={axis: lax.rem(own + j, size)})

    loads = [
        pltpu.make_async_copy(source, target, load_sem.at[i])
        for i, (source, target) in enumerate(
            (
                (order_hbm, order),
                (coords_hbm, coords),
                (noise_hbm, noise),
                (probes_hbm, probes),
                (factors_hbm.at[:, 1], right),
            )
        )
    ]
    for load in loads:
        load.start()

    def send(step, source, target, axis, peer):
        pltpu.make_async_remote_copy(
            src_ref=source,
            dst_ref=target,
            send_sem=send_sem.at[step],
            recv_sem=recv_sem.at[step],
            device_id={axis: peer},
        ).start()

    def wait_all(sems, step, ref, count):
        whole = ref.at[pl.ds(0, count)]
        pltpu.make_async_copy(whole, whole, sems.at[step]).wait()

    loads[0].wait()
    wanted = order[...]
    source = ((wanted >> (points.bit_length() - 1)) - gy) & (inner - 1)
    local_index = wanted & (points - 1)
    kind = lax.broadcasted_iota(jnp.int32, (inner, TILE), 0)
    chunks = points // TILE
    for k in range(chunks):
        counts[k * inner : (k + 1) * inner, :] = (
            kind == source[:, k * TILE : (k + 1) * TILE]
        ).astype(jnp.bfloat16)
    before = lax.broadcasted_iota(jnp.int32, (TILE, 2 * TILE), 0)
    column = lax.broadcasted_iota(jnp.int32, (TILE, 2 * TILE), 1)
    ones = ((before < column) | (column >= TILE)).astype(jnp.bfloat16)
    ahead = dot(counts[...], ones)
    offset = jnp.zeros((inner, TILE), jnp.float32)
    for k in range(chunks):
        rows = ahead[k * inner : (k + 1) * inner]
        own_source = source[:, k * TILE : (k + 1) * TILE]
        place = jnp.sum(
            jnp.where(kind == own_source, rows[:, :TILE] + offset, 0.0), axis=0, keepdims=True
        )
        slots[:, k * TILE : (k + 1) * TILE] = own_source * slot + place.astype(jnp.int32)
        offset = offset + rows[:, TILE:]

    place = slots[...]
    upper = lax.broadcasted_iota(jnp.int32, (points // LANES, points), 0) == (place >> 7)
    lower = lax.broadcasted_iota(jnp.int32, (LANES, points), 0) == (place & (LANES - 1))
    low_part = (local_index & 63).astype(jnp.float32)
    high_part = (local_index >> 6).astype(jnp.float32)
    marked = jnp.concatenate(
        [jnp.where(upper, low_part, 0.0), jnp.where(upper, high_part, 0.0)], axis=0
    ).astype(jnp.bfloat16)
    lists = dot(marked, lower.astype(jnp.bfloat16), NT)
    lists = (lists[: points // LANES] + 64.0 * lists[points // LANES :]).astype(jnp.int32)
    for j in range(inner):
        ask[j] = lists[2 * j : 2 * j + 2]

    pl.semaphore_wait(barrier, inner + outer - 2)

    @pl.loop(1, inner)
    def _(j):
        send(0, ask.at[j], asked.at[j - 1], "gy", lax.rem(gy + j, inner))

    loads[3].wait()
    loads[4].wait()
    vectors = probes[...]
    coeff = dot(vectors, right[2:].reshape(far * RANK, points), NT)
    for k in range(inner):
        part[k] = coeff[k * share : (k + 1) * share]
    parts[pl.ds(gy, 1)] = part[pl.ds(gy, 1)]

    @pl.loop(1, inner)
    def _(j):
        peer = lax.rem(gy + j, inner)
        send(2, part.at[peer], parts.at[gy], "gy", peer)

    loads[1].wait()
    loads[2].wait()
    values = jnp.concatenate([coords[...], noise[...]], axis=0)
    vectors_own = [
        jnp.concatenate(
            [values[:, c * LANES : (c + 1) * LANES] for c in (2 * r, 2 * r + 1)], axis=0
        )
        for r in range(points // TILE)
    ]
    for r in range(points // TILE):
        table[r] = vectors_own[r]

    near = [
        dot(
            vectors[:, a * LEAF : (a + 1) * LEAF],
            right[:2, :, a * LEAF : (a + 1) * LEAF].reshape(2 * RANK, LEAF),
            NT,
        )
        for a in range(points // LEAF)
    ]
    level = lax.broadcasted_iota(jnp.int32, (PROBES, 2 * RANK), 1) < RANK
    for a in range(points // LEAF):
        other = 2 * (1 - a // 2)
        near_ref[a] = jnp.where(level, near[a ^ 1], near[other] + near[other + 1]).astype(
            jnp.bfloat16
        )

    own_table = [table[r] for r in range(points // TILE)]
    given[0] = look_up(own_table, ask[0, 0:1], ask[0, 1:2])
    wait_all(recv_sem, 0, asked, inner - 1)

    @pl.loop(1, inner)
    def _(j):
        own_table = [table[r] for r in range(points // TILE)]
        lists = asked[j - 1]
        give[j - 1] = look_up(own_table, lists[0:1], lists[1:2])
        send(1, give.at[j - 1], given.at[j], "gy", lax.rem(gy - j + inner, inner))

    wait_all(recv_sem, 2, parts, inner - 1)
    half = inner_bits * RANK
    lane = lax.broadcasted_iota(jnp.int32, (share, half), 1)
    sums = [[parts[e] for e in range(inner)]]
    for step in range(inner_bits):
        last = sums[-1]
        sums.append([last[2 * g] + last[2 * g + 1] for g in range(len(last) // 2)])
    total[...] = sums[inner_bits][0][:, half:]
    totals[pl.ds(gx, 1)] = total[...][None]

    @pl.loop(1, outer)
    def _(j):
        send(3, total, totals.at[gx], "gx", lax.rem(gx + j, outer))

    for d in range(inner):
        picked = sums[inner_bits - 1][(d >> (inner_bits - 1)) ^ 1][:, :half]
        for h in reversed(range(inner_bits - 1)):
            picked = jnp.where(lane < (h + 1) * RANK, sums[h][(d >> h) ^ 1][:, :half], picked)
        inner_sib[d] = picked

    wait_all(recv_sem, 1, given, inner - 1)
    received = [given[r] for r in range(inner)]
    for k in range(chunks):
        found = look_up(
            received,
            slots[:, 2 * k * LANES : (2 * k + 1) * LANES],
            slots[:, (2 * k + 1) * LANES : (2 * k + 2) * LANES],
        )
        tree_ref[:, 2 * k * LANES : (2 * k + 1) * LANES] = found[0:4]
        tree_ref[:, (2 * k + 1) * LANES : (2 * k + 2) * LANES] = found[4:8]

    wait_all(recv_sem, 3, totals, outer - 1)
    width = outer_bits * RANK
    lane = lax.broadcasted_iota(jnp.int32, (share, width), 1)
    base = 0
    sums = [totals[e] for e in range(outer)]
    picked = None
    for h in range(outer_bits):
        for g, value in enumerate(sums):
            pairs[base + g] = value
        group = gx // 2**h
        sibling = pairs[base + group + 1 - 2 * (group % 2)]
        picked = sibling if picked is None else jnp.where(lane < h * RANK, picked, sibling)
        base += len(sums)
        sums = [sums[2 * g] + sums[2 * g + 1] for g in range(len(sums) // 2)]
    for d in range(inner):
        back[d] = jnp.concatenate([inner_sib[d], picked], axis=1)
    backs[pl.ds(gy, 1)] = back[pl.ds(gy, 1)]

    @pl.loop(1, inner)
    def _(j):
        peer = lax.rem(gy + j, inner)
        send(4, back.at[peer], backs.at[gy], "gy", peer)

    wait_all(recv_sem, 4, backs, inner - 1)
    sib_ref[...] = jnp.concatenate([backs[k] for k in range(inner)], axis=0).astype(jnp.bfloat16)

    wait_all(send_sem, 0, asked, inner - 1)
    wait_all(send_sem, 1, give, inner - 1)
    wait_all(send_sem, 2, part, inner - 1)
    wait_all(send_sem, 3, totals, outer - 1)
    wait_all(send_sem, 4, back, inner - 1)


def exchange(inner, outer, coords, noise, order, probes, factors):
    points = probes.shape[1]
    levels = factors.shape[0]
    far = levels - 2
    share = PROBES // inner
    inner_bits = inner.bit_length() - 1
    outer_bits = outer.bit_length() - 1
    wide = far * RANK
    f32, bf16, i32 = jnp.float32, jnp.bfloat16, jnp.int32
    hbm = pl.BlockSpec(memory_space=pl.ANY)
    vmem = pl.BlockSpec(memory_space=pltpu.VMEM)
    return pl.pallas_call(
        functools.partial(exchange_kernel, inner, outer),
        out_shape=(
            jax.ShapeDtypeStruct((4, points), f32),
            jax.ShapeDtypeStruct((PROBES, wide), bf16),
            jax.ShapeDtypeStruct((points // LEAF, PROBES, 2 * RANK), bf16),
        ),
        in_specs=[hbm] * 5,
        out_specs=(vmem, vmem, vmem),
        scratch_shapes=[
            pltpu.VMEM((3, points), f32),
            pltpu.VMEM((1, points), f32),
            pltpu.VMEM((1, points), i32),
            pltpu.VMEM((PROBES, points), bf16),
            pltpu.VMEM((levels, RANK, points), bf16),
            pltpu.VMEM((inner * points // TILE, TILE), bf16),
            pltpu.VMEM((1, points), i32),
            pltpu.VMEM((points // TILE, 8, LANES), f32),
            pltpu.VMEM((inner, 2, LANES), i32),
            pltpu.VMEM((inner - 1, 2, LANES), i32),
            pltpu.VMEM((inner - 1, 8, LANES), f32),
            pltpu.VMEM((inner, 8, LANES), f32),
            pltpu.VMEM((inner, share, wide), f32),
            pltpu.VMEM((inner, share, wide), f32),
            pltpu.VMEM((inner, share, inner_bits * RANK), f32),
            pltpu.VMEM((share, outer_bits * RANK), f32),
            pltpu.VMEM((outer, share, outer_bits * RANK), f32),
            pltpu.VMEM((2 * outer, share, outer_bits * RANK), f32),
            pltpu.VMEM((inner, share, wide), f32),
            pltpu.VMEM((inner, share, wide), f32),
            pltpu.SemaphoreType.DMA((5,)),
            pltpu.SemaphoreType.DMA((5,)),
            pltpu.SemaphoreType.DMA((5,)),
        ],
        compiler_params=pltpu.CompilerParams(
            collective_id=0, has_side_effects=True, vmem_limit_bytes=40 * 2**20
        ),
    )(coords, noise.reshape(1, points), order, probes, factors)


def split_three(x):
    one = x.astype(jnp.bfloat16)
    rest = x - one.astype(jnp.float32)
    two = rest.astype(jnp.bfloat16)
    three = (rest - two.astype(jnp.float32)).astype(jnp.bfloat16)
    return one.astype(jnp.float32), two.astype(jnp.float32), three.astype(jnp.float32)


def leaf_kernel(tree_ref, sib_ref, near_ref, probes_ref, left_ref, out_ref, one_ref, two_ref):
    spots = (tree_ref[0:3, :] - 4.0) * SQRT_THREE
    norm = spots * spots
    norm = norm[0:1] + norm[1:2] + norm[2:3]
    a, b, c = split_three(spots)
    n1, n2, n3 = split_three(norm)
    unit = jnp.ones_like(norm)
    pad = jnp.zeros((8, LEAF), jnp.float32)
    one_ref[...] = jnp.concatenate(
        [a, a, b, a, c, b, n1, n2, n3, unit, unit, unit, pad], axis=0
    ).astype(jnp.bfloat16)
    two_ref[...] = jnp.concatenate(
        [-2.0 * v for v in (a, b, a, c, a, b)] + [unit, unit, unit, n1, n2, n3, pad], axis=0
    ).astype(jnp.bfloat16)

    levels = left_ref.shape[0]
    left = left_ref[...].reshape(levels * RANK, LEAF)
    out_ref[...] = dot(near_ref[0], left[: 2 * RANK]) + dot(sib_ref[...], left[2 * RANK :])
    eye = lax.broadcasted_iota(jnp.int32, (TILE, TILE), 0) == lax.broadcasted_iota(
        jnp.int32, (TILE, TILE), 1
    )
    tiles = LEAF // TILE
    for i in range(tiles):
        for j in range(i, tiles):
            rows = pl.ds(i * TILE, TILE)
            columns = pl.ds(j * TILE, TILE)
            square = jnp.maximum(dot(one_ref[:, rows], two_ref[:, columns], TN), 1e-30)
            scaled = square * lax.rsqrt(square)
            block = (1.0 + scaled) * jnp.exp(-scaled)
            if i == j:
                block = jnp.where(eye, 1.0 + tree_ref[3:4, rows], block)
            block = block.astype(jnp.bfloat16)
            out_ref[:, columns] += dot(probes_ref[:, rows], block)
            if i != j:
                out_ref[:, rows] += dot(probes_ref[:, columns], block, NT)


def leaves(tree, sib, near, probes, factors):
    points = probes.shape[1]
    levels = factors.shape[0]
    return pl.pallas_call(
        leaf_kernel,
        grid=(points // LEAF,),
        out_shape=jax.ShapeDtypeStruct((PROBES, points), jnp.float32),
        in_specs=[
            pl.BlockSpec((4, LEAF), lambda i: (0, i)),
            pl.BlockSpec(sib.shape, lambda i: (0, 0)),
            pl.BlockSpec((1, PROBES, 2 * RANK), lambda i: (i, 0, 0)),
            pl.BlockSpec((PROBES, LEAF), lambda i: (0, i)),
            pl.BlockSpec((levels, None, RANK, LEAF), lambda i: (0, 0, 0, i)),
        ],
        out_specs=pl.BlockSpec((PROBES, LEAF), lambda i: (0, i)),
        scratch_shapes=[
            pltpu.VMEM((32, LEAF), jnp.bfloat16),
            pltpu.VMEM((32, LEAF), jnp.bfloat16),
        ],
        compiler_params=pltpu.CompilerParams(vmem_limit_bytes=40 * 2**20),
    )(tree, sib, near, probes, factors)


def solution(mesh):
    inner, outer = mesh.shape["gy"], mesh.shape["gx"]

    def local(coords, noise, order, probes, factors):
        tree, sib, near = exchange(inner, outer, coords, noise, order, probes, factors)
        return leaves(tree, sib, near, probes, factors)

    return jax.shard_map(
        local,
        mesh=mesh,
        in_specs=(
            P(None, ("gx", "gy")),
            P(("gx", "gy")),
            P("gx", "gy"),
            P(None, ("gx", "gy")),
            P(None, None, None, ("gx", "gy")),
        ),
        out_specs=P(None, ("gx", "gy")),
        check_vma=False,
    )
```

```python
import functools

import jax
import jax.numpy as jnp
from jax import lax
from jax.experimental import pallas as pl
from jax.experimental.pallas import tpu as pltpu
from jax.sharding import PartitionSpec as P

LEAF = 1024
RANK = 32
PROBES = 64
LANES = 128
TILE = 256
NT = (((1,), (1,)), ((), ()))
SQRT_THREE = 1.7320508075688772
LOG2_E = 1.4426950408889634


def dot(a, b, dims=(((1,), (0,)), ((), ()))):
    return lax.dot_general(a, b, dims, preferred_element_type=jnp.float32)


def look_up(table, first, second):
    shape = (8, LANES)
    found = []
    for picks in (first, second):
        picks = jnp.broadcast_to(picks, shape)
        lane = picks & (LANES - 1)
        upper = picks >> 8
        out = jnp.zeros(shape, jnp.float32)
        for r, vector in enumerate(table):
            out = jnp.where(
                upper == r,
                jnp.take_along_axis(vector, lane, axis=1, mode="promise_in_bounds"),
                out,
            )
        found.append((out, ((picks >> 7) & 1) == 0))
    row = lax.broadcasted_iota(jnp.int32, shape, 0)
    (one, one_low), (two, two_low) = found
    return jnp.where(
        row < 4,
        jnp.where(one_low, one, pltpu.roll(one, 4, 0)),
        jnp.where(two_low, pltpu.roll(two, 4, 0), two),
    )


def split_three(x):
    one = x.astype(jnp.bfloat16)
    rest = x - one.astype(jnp.float32)
    two = rest.astype(jnp.bfloat16)
    three = (rest - two.astype(jnp.float32)).astype(jnp.bfloat16)
    return one.astype(jnp.float32), two.astype(jnp.float32), three.astype(jnp.float32)


def far_first(step, size):
    odd = lax.rem(step, 2)
    return size // 2 + odd * ((step + 1) // 2) - (1 - odd) * (step // 2)


def leaf_features(values):
    spots = (values[0:3] - 4.0) * SQRT_THREE
    norm = spots * spots
    norm = norm[0:1] + norm[1:2] + norm[2:3]
    a, b, c = split_three(spots)
    n1, n2, n3 = split_three(norm)
    unit = jnp.ones_like(norm)
    pad = jnp.zeros((8, norm.shape[1]), jnp.float32)
    one = jnp.concatenate([a, a, b, a, c, b, n1, n2, n3, unit, unit, unit, pad], axis=0)
    two = jnp.concatenate(
        [-2.0 * v for v in (a, b, a, c, a, b)] + [unit, unit, unit, n1, n2, n3, pad], axis=0
    )
    return one.astype(jnp.bfloat16), two.astype(jnp.bfloat16)


def matern(square):
    square = jnp.maximum(square, 1e-30)
    scaled = square * lax.rsqrt(square)
    return (1.0 + scaled) * jnp.exp2(scaled * -LOG2_E)


def leaf_product(tree, probes, one_ref, two_ref, block_ref, out_ref, start):
    values = tree[:, pl.ds(start, LEAF)]
    one, two = leaf_features(values)
    one_ref[...] = one.T
    two_ref[...] = two
    half = TILE // 2
    eye = lax.broadcasted_iota(jnp.int32, (half, half), 0) == lax.broadcasted_iota(
        jnp.int32, (half, half), 1
    )
    tiles = LEAF // TILE
    for j in range(tiles):
        first, middle, last = j * TILE, j * TILE + half, (j + 1) * TILE
        if j:
            block_ref[:first, first:last] = matern(
                dot(one_ref[:first], two_ref[:, first:last])
            ).astype(jnp.bfloat16)
        upper = matern(dot(one_ref[first:middle], two_ref[:, first:last]))
        side = upper[:, half:].astype(jnp.bfloat16)
        block_ref[first:middle, first:middle] = jnp.where(
            eye, 1.0 + values[3:4, first:middle], upper[:, :half]
        ).astype(jnp.bfloat16)
        block_ref[first:middle, middle:last] = side
        block_ref[middle:last, first:middle] = side.T
        block_ref[middle:last, middle:last] = jnp.where(
            eye,
            1.0 + values[3:4, middle:last],
            matern(dot(one_ref[middle:last], two_ref[:, middle:last])),
        ).astype(jnp.bfloat16)
    for j in range(tiles):
        first, last = j * TILE, (j + 1) * TILE
        columns = pl.ds(start + first, TILE)
        total = out_ref[:, columns] + dot(
            probes[:, pl.ds(start, last)], block_ref[:last, first:last]
        )
        if j < tiles - 1:
            total = total + dot(
                probes[:, pl.ds(start + last, LEAF - last)], block_ref[first:last, last:], NT
            )
        out_ref[:, columns] = total


def exchange_kernel(
    inner,
    outer,
    coords_hbm,
    noise_hbm,
    order_hbm,
    probes_hbm,
    factors_hbm,
    dense_ref,
    sib_ref,
    left_ref,
    coords,
    noise,
    order,
    probes,
    right,
    beside,
    tree,
    one_ref,
    two_ref,
    block_ref,
    counts,
    slots,
    table,
    ask,
    asked,
    give,
    given,
    part,
    parts,
    inner_sib,
    total,
    totals,
    pairs,
    back,
    backs,
    load_sem,
    send_sem,
    recv_sem,
):
    gx, gy = lax.axis_index("gx"), lax.axis_index("gy")
    points = order.shape[1]
    slot = points // inner
    levels = right.shape[0]
    far = levels - 2
    inner_bits = inner.bit_length() - 1
    outer_bits = outer.bit_length() - 1
    share = PROBES // inner

    barrier = pltpu.get_barrier_semaphore()
    for axis, own, size in (("gy", gy, inner), ("gx", gx, outer)):

        @pl.loop(1, size)
        def _(j):
            pl.semaphore_signal(barrier, inc=1, device_id={axis: lax.rem(own + j, size)})

    loads = [
        pltpu.make_async_copy(source, target, load_sem.at[i])
        for i, (source, target) in enumerate(
            (
                (order_hbm, order),
                (coords_hbm, coords),
                (noise_hbm, noise),
                (probes_hbm, probes),
                (factors_hbm.at[2:, 1], right.at[2:]),
                (factors_hbm.at[:2, 1], right.at[:2]),
                (factors_hbm.at[:2, 0], beside),
                (factors_hbm.at[2:, 0], left_ref),
            )
        )
    ]
    for load in loads[:5]:
        load.start()

    def send(step, source, target, axis, peer):
        pltpu.make_async_remote_copy(
            src_ref=source,
            dst_ref=target,
            send_sem=send_sem.at[step],
            recv_sem=recv_sem.at[step],
            device_id={axis: peer},
        ).start()

    def wait_all(sems, step, ref, first, count):
        whole = ref.at[pl.ds(first, count)]
        pltpu.make_async_copy(whole, whole, sems.at[step]).wait()

    loads[0].wait()
    wanted = order[...]
    source = ((wanted >> (points.bit_length() - 1)) - gy) & (inner - 1)
    local_index = wanted & (points - 1)
    kind = lax.broadcasted_iota(jnp.int32, (inner, TILE), 0)
    chunks = points // TILE
    for k in range(chunks):
        counts[k * inner : (k + 1) * inner, :] = (
            kind == source[:, k * TILE : (k + 1) * TILE]
        ).astype(jnp.bfloat16)
    before = lax.broadcasted_iota(jnp.int32, (TILE, 2 * TILE), 0)
    column = lax.broadcasted_iota(jnp.int32, (TILE, 2 * TILE), 1)
    ones = ((before < column) | (column >= TILE)).astype(jnp.bfloat16)
    ahead = dot(counts[...], ones)
    offset = jnp.zeros((inner, TILE), jnp.float32)
    for k in range(chunks):
        rows = ahead[k * inner : (k + 1) * inner]
        own_source = source[:, k * TILE : (k + 1) * TILE]
        place = jnp.sum(
            jnp.where(kind == own_source, rows[:, :TILE] + offset, 0.0), axis=0, keepdims=True
        )
        slots[:, k * TILE : (k + 1) * TILE] = own_source * slot + place.astype(jnp.int32)
        offset = offset + rows[:, TILE:]

    place = slots[...]
    upper = lax.broadcasted_iota(jnp.int32, (points // LANES, points), 0) == (place >> 7)
    lower = lax.broadcasted_iota(jnp.int32, (LANES, points), 0) == (place & (LANES - 1))
    low_part = (local_index & 63).astype(jnp.float32)
    high_part = (local_index >> 6).astype(jnp.float32)
    marked = jnp.concatenate(
        [jnp.where(upper, low_part, 0.0), jnp.where(upper, high_part, 0.0)], axis=0
    ).astype(jnp.bfloat16)
    lists = dot(marked, lower.astype(jnp.bfloat16), NT)
    lists = (lists[: points // LANES] + 64.0 * lists[points // LANES :]).astype(jnp.int32)
    for j in range(inner):
        ask[j] = lists[2 * j : 2 * j + 2]

    pl.semaphore_wait(barrier, inner + outer - 2)

    @pl.loop(0, inner - 1)
    def _(step):
        j = far_first(step, inner)
        send(0, ask.at[j], asked.at[j], "gy", lax.rem(gy + j, inner))

    loads[3].wait()
    loads[4].wait()
    vectors = probes[...]
    coeff = dot(vectors, right[2:].reshape(far * RANK, points), NT)
    for k in range(inner):
        part[k] = coeff[k * share : (k + 1) * share]
    parts[pl.ds(gy, 1)] = part[pl.ds(gy, 1)]

    @pl.loop(0, inner - 1)
    def _(step):
        peer = lax.rem(gy + far_first(step, inner), inner)
        send(2, part.at[peer], parts.at[gy], "gy", peer)

    for load in loads[5:]:
        load.start()
    loads[1].wait()
    loads[2].wait()
    values = jnp.concatenate([coords[...], noise[...]], axis=0)
    vectors_own = [
        jnp.concatenate(
            [values[:, c * LANES : (c + 1) * LANES] for c in (2 * r, 2 * r + 1)], axis=0
        )
        for r in range(points // TILE)
    ]
    for r in range(points // TILE):
        table[r] = vectors_own[r]

    given[0] = look_up(vectors_own, ask[0, 0:1], ask[0, 1:2])

    loads[5].wait()
    loads[6].wait()
    near = [
        dot(
            vectors[:, a * LEAF : (a + 1) * LEAF],
            right[:2, :, a * LEAF : (a + 1) * LEAF].reshape(2 * RANK, LEAF),
            NT,
        )
        for a in range(points // LEAF)
    ]
    level = lax.broadcasted_iota(jnp.int32, (PROBES, 2 * RANK), 1) < RANK
    for a in range(points // LEAF):
        other = 2 * (1 - a // 2)
        sibling = jnp.where(level, near[a ^ 1], near[other] + near[other + 1])
        dense_ref[:, a * LEAF : (a + 1) * LEAF] = dot(
            sibling.astype(jnp.bfloat16),
            beside[:, :, a * LEAF : (a + 1) * LEAF].reshape(2 * RANK, LEAF),
        )

    wait_all(recv_sem, 0, asked, 1, inner - 1)

    @pl.loop(0, inner - 1)
    def _(step):
        j = far_first(step, inner)
        own_table = [table[r] for r in range(points // TILE)]
        lists = asked[j]
        give[j] = look_up(own_table, lists[0:1], lists[1:2])
        send(1, give.at[j], given.at[j], "gy", lax.rem(gy - j + inner, inner))

    wait_all(recv_sem, 2, parts, 0, inner - 1)
    half = inner_bits * RANK
    lane = lax.broadcasted_iota(jnp.int32, (share, half), 1)
    sums = [[parts[e] for e in range(inner)]]
    for step in range(inner_bits):
        last = sums[-1]
        sums.append([last[2 * g] + last[2 * g + 1] for g in range(len(last) // 2)])
    total[...] = sums[inner_bits][0][:, half:]
    totals[pl.ds(gx, 1)] = total[...][None]

    @pl.loop(1, outer)
    def _(j):
        send(3, total, totals.at[gx], "gx", lax.rem(gx + j, outer))

    for d in range(inner):
        picked = sums[inner_bits - 1][(d >> (inner_bits - 1)) ^ 1][:, :half]
        for h in reversed(range(inner_bits - 1)):
            picked = jnp.where(lane < (h + 1) * RANK, sums[h][(d >> h) ^ 1][:, :half], picked)
        inner_sib[d] = picked

    wait_all(recv_sem, 3, totals, 0, outer - 1)
    width = outer_bits * RANK
    lane = lax.broadcasted_iota(jnp.int32, (share, width), 1)
    base = 0
    sums = [totals[e] for e in range(outer)]
    picked = None
    for h in range(outer_bits):
        for g, value in enumerate(sums):
            pairs[base + g] = value
        group = gx // 2**h
        sibling = pairs[base + group + 1 - 2 * (group % 2)]
        picked = sibling if picked is None else jnp.where(lane < h * RANK, picked, sibling)
        base += len(sums)
        sums = [sums[2 * g] + sums[2 * g + 1] for g in range(len(sums) // 2)]
    for d in range(inner):
        back[d] = jnp.concatenate([inner_sib[d], picked], axis=1)
    backs[pl.ds(gy, 1)] = back[pl.ds(gy, 1)]

    @pl.loop(0, inner - 1)
    def _(step):
        peer = lax.rem(gy + far_first(step, inner), inner)
        send(4, back.at[peer], backs.at[gy], "gy", peer)

    wait_all(recv_sem, 1, given, 1, inner - 1)
    received = [given[r] for r in range(inner)]
    for k in range(chunks):
        found = look_up(
            received,
            slots[:, 2 * k * LANES : (2 * k + 1) * LANES],
            slots[:, (2 * k + 1) * LANES : (2 * k + 2) * LANES],
        )
        tree[:, 2 * k * LANES : (2 * k + 1) * LANES] = found[0:4]
        tree[:, (2 * k + 1) * LANES : (2 * k + 2) * LANES] = found[4:8]

    @pl.loop(0, points // LEAF)
    def _(a):
        leaf_product(
            tree,
            probes,
            one_ref,
            two_ref,
            block_ref,
            dense_ref,
            pl.multiple_of(a * LEAF, LEAF),
        )

    wait_all(recv_sem, 4, backs, 0, inner - 1)
    sib_ref[...] = jnp.concatenate([backs[k] for k in range(inner)], axis=0).astype(jnp.bfloat16)

    loads[7].wait()
    wait_all(send_sem, 0, ask, 1, inner - 1)
    wait_all(send_sem, 1, give, 1, inner - 1)
    wait_all(send_sem, 2, part, 0, inner - 1)
    wait_all(send_sem, 3, totals, 0, outer - 1)
    wait_all(send_sem, 4, back, 0, inner - 1)


def exchange(inner, outer, coords, noise, order, probes, factors):
    points = probes.shape[1]
    levels = factors.shape[0]
    far = levels - 2
    share = PROBES // inner
    inner_bits = inner.bit_length() - 1
    outer_bits = outer.bit_length() - 1
    wide = far * RANK
    f32, bf16, i32 = jnp.float32, jnp.bfloat16, jnp.int32
    hbm = pl.BlockSpec(memory_space=pltpu.HBM)
    vmem = pl.BlockSpec(memory_space=pltpu.VMEM)
    return pl.pallas_call(
        functools.partial(exchange_kernel, inner, outer),
        out_shape=(
            jax.ShapeDtypeStruct((PROBES, points), f32),
            jax.ShapeDtypeStruct((PROBES, wide), bf16),
            jax.ShapeDtypeStruct((far, RANK, points), bf16),
        ),
        in_specs=[hbm] * 5,
        out_specs=(vmem, vmem, vmem),
        scratch_shapes=[
            pltpu.VMEM((3, points), f32),
            pltpu.VMEM((1, points), f32),
            pltpu.VMEM((1, points), i32),
            pltpu.VMEM((PROBES, points), bf16),
            pltpu.VMEM((levels, RANK, points), bf16),
            pltpu.VMEM((2, RANK, points), bf16),
            pltpu.VMEM((4, points), f32),
            pltpu.VMEM((LEAF, 32), bf16),
            pltpu.VMEM((32, LEAF), bf16),
            pltpu.VMEM((LEAF, LEAF), bf16),
            pltpu.VMEM((inner * points // TILE, TILE), bf16),
            pltpu.VMEM((1, points), i32),
            pltpu.VMEM((points // TILE, 8, LANES), f32),
            pltpu.VMEM((inner, 2, LANES), i32),
            pltpu.VMEM((inner, 2, LANES), i32),
            pltpu.VMEM((inner, 8, LANES), f32),
            pltpu.VMEM((inner, 8, LANES), f32),
            pltpu.VMEM((inner, share, wide), f32),
            pltpu.VMEM((inner, share, wide), f32),
            pltpu.VMEM((inner, share, inner_bits * RANK), f32),
            pltpu.VMEM((share, outer_bits * RANK), f32),
            pltpu.VMEM((outer, share, outer_bits * RANK), f32),
            pltpu.VMEM((2 * outer, share, outer_bits * RANK), f32),
            pltpu.VMEM((inner, share, wide), f32),
            pltpu.VMEM((inner, share, wide), f32),
            pltpu.SemaphoreType.DMA((8,)),
            pltpu.SemaphoreType.DMA((5,)),
            pltpu.SemaphoreType.DMA((5,)),
        ],
        compiler_params=pltpu.CompilerParams(
            collective_id=0, has_side_effects=True, vmem_limit_bytes=40 * 2**20
        ),
    )(
        *(
            pltpu.with_memory_space_constraint(array, pltpu.HBM)
            for array in (coords, noise.reshape(1, points), order, probes, factors)
        )
    )


def expand_kernel(dense, sib, left, out_hbm, result, sems):
    points = dense.shape[1]
    width = result.shape[2]
    writes = []
    for c in range(points // width):
        columns = slice(c * width, (c + 1) * width)
        result[c] = dense[:, columns] + dot(
            sib[...], left[:, :, columns].reshape(sib.shape[1], width)
        )
        writes.append(
            pltpu.make_async_copy(result.at[c], out_hbm.at[:, columns], sems.at[c])
        )
        writes[-1].start()
    for write in writes:
        write.wait()


def expand(dense, sib, left):
    points = dense.shape[1]
    width = 512
    vmem = pl.BlockSpec(memory_space=pltpu.VMEM)
    return pl.pallas_call(
        expand_kernel,
        out_shape=jax.ShapeDtypeStruct((PROBES, points), jnp.float32),
        in_specs=[vmem] * 3,
        out_specs=pl.BlockSpec(memory_space=pltpu.HBM),
        scratch_shapes=[
            pltpu.VMEM((points // width, PROBES, width), jnp.float32),
            pltpu.SemaphoreType.DMA((points // width,)),
        ],
        compiler_params=pltpu.CompilerParams(vmem_limit_bytes=16 * 2**20),
    )(dense, sib, left)


def solution(mesh):
    inner, outer = mesh.shape["gy"], mesh.shape["gx"]

    def local(coords, noise, order, probes, factors):
        return expand(*exchange(inner, outer, coords, noise, order, probes, factors))

    return jax.shard_map(
        local,
        mesh=mesh,
        in_specs=(
            P(None, ("gx", "gy")),
            P(("gx", "gy")),
            P("gx", "gy"),
            P(None, ("gx", "gy")),
            P(None, None, None, ("gx", "gy")),
        ),
        out_specs=P(None, ("gx", "gy")),
        check_vma=False,
    )
```

```python
import functools

import jax
import jax.numpy as jnp
from jax import lax
from jax.experimental import pallas as pl
from jax.experimental.pallas import tpu as pltpu
from jax.sharding import PartitionSpec as P

LEAF = 1024
RANK = 32
PROBES = 64
LANES = 128
TILE = 256
OWNERS = 8
NT = (((1,), (1,)), ((), ()))
SQRT_THREE = 1.7320508075688772
LOG2_E = 1.4426950408889634


def dot(a, b, dims=(((1,), (0,)), ((), ()))):
    return lax.dot_general(a, b, dims, preferred_element_type=jnp.float32)


def look_up(table, first, second):
    shape = (8, LANES)
    found = []
    for picks in (first, second):
        picks = jnp.broadcast_to(picks, shape)
        lane = picks & (LANES - 1)
        upper = picks >> 8
        out = jnp.zeros(shape, jnp.float32)
        for r, vector in enumerate(table):
            out = jnp.where(
                upper == r,
                jnp.take_along_axis(vector, lane, axis=1, mode="promise_in_bounds"),
                out,
            )
        found.append((out, ((picks >> 7) & 1) == 0))
    row = lax.broadcasted_iota(jnp.int32, shape, 0)
    (one, one_low), (two, two_low) = found
    return jnp.where(
        row < 4,
        jnp.where(one_low, one, pltpu.roll(one, 4, 0)),
        jnp.where(two_low, pltpu.roll(two, 4, 0), two),
    )


def split_three(x):
    one = x.astype(jnp.bfloat16)
    rest = x - one.astype(jnp.float32)
    two = rest.astype(jnp.bfloat16)
    three = (rest - two.astype(jnp.float32)).astype(jnp.bfloat16)
    return one.astype(jnp.float32), two.astype(jnp.float32), three.astype(jnp.float32)


def far_first(step, size):
    odd = lax.rem(step, 2)
    return size // 2 + odd * ((step + 1) // 2) - (1 - odd) * (step // 2)


def leaf_features(values):
    spots = (values[0:3] - 4.0) * SQRT_THREE
    norm = spots * spots
    norm = norm[0:1] + norm[1:2] + norm[2:3]
    a, b, c = split_three(spots)
    n1, n2, n3 = split_three(norm)
    unit = jnp.ones_like(norm)
    pad = jnp.zeros((8, norm.shape[1]), jnp.float32)
    one = jnp.concatenate([a, a, b, a, c, b, n1, n2, n3, unit, unit, unit, pad], axis=0)
    two = jnp.concatenate(
        [-2.0 * v for v in (a, b, a, c, a, b)] + [unit, unit, unit, n1, n2, n3, pad], axis=0
    )
    return one.astype(jnp.bfloat16), two.astype(jnp.bfloat16)


def matern(square):
    scaled = square * lax.rsqrt(jnp.maximum(square, 1e-3))
    return (1.0 + scaled) * jnp.exp2(scaled * -LOG2_E)


def leaf_products(given, slots, probes, even, odd, out_ref):
    points = slots.shape[1]
    half = TILE // 2
    tiles = LEAF // TILE

    def multiply(leaf, block_ref):
        start = leaf * LEAF
        for j in range(tiles):
            first, last = j * TILE, (j + 1) * TILE
            columns = pl.ds(pl.multiple_of(start + first, TILE), TILE)
            total = out_ref[:, columns] + dot(
                probes[:, pl.ds(pl.multiple_of(start, TILE), last)], block_ref[:last, first:last]
            )
            if j < tiles - 1:
                rest = pl.ds(pl.multiple_of(start + last, TILE), LEAF - last)
                total = total + dot(probes[:, rest], block_ref[first:last, last:], NT)
            out_ref[:, columns] = total

    def find(leaf, j, noise_ref, one_ref, two_ref, block_ref):
        at = leaf * LEAF + j * TILE
        found = look_up(
            [given[r] for r in range(given.shape[0])],
            slots[:, pl.ds(pl.multiple_of(at, LANES), LANES)],
            slots[:, pl.ds(pl.multiple_of(at + LANES, LANES), LANES)],
        )
        columns = slice(j * TILE, (j + 1) * TILE)
        values = jnp.concatenate([found[0:4], found[4:8]], axis=1)
        one, two = leaf_features(values)
        one_ref[columns, :] = one.T
        two_ref[:, columns] = two
        noise_ref[:, columns] = 1.0 + values[3:4]

    def fill(j, noise_ref, one_ref, two_ref, block_ref):
        first, middle, last = j * TILE, j * TILE + half, (j + 1) * TILE
        eye = lax.broadcasted_iota(jnp.int32, (half, half), 0) == lax.broadcasted_iota(
            jnp.int32, (half, half), 1
        )
        if j:
            block_ref[:first, first:last] = matern(
                dot(one_ref[:first], two_ref[:, first:last])
            ).astype(jnp.bfloat16)
        upper = matern(dot(one_ref[first:middle], two_ref[:, first:last]))
        side = upper[:, half:].astype(jnp.bfloat16)
        block_ref[first:middle, first:middle] = jnp.where(
            eye, noise_ref[:, first:middle], upper[:, :half]
        ).astype(jnp.bfloat16)
        block_ref[first:middle, middle:last] = side
        block_ref[middle:last, first:middle] = side.T
        block_ref[middle:last, middle:last] = jnp.where(
            eye,
            noise_ref[:, middle:last],
            matern(dot(one_ref[middle:last], two_ref[:, middle:last])),
        ).astype(jnp.bfloat16)

    leaves = points // LEAF

    sets = (even, odd)
    for j in range(tiles):
        find(0, j, *even)
    for leaf in range(leaves):
        now, later = sets[leaf % 2], sets[(leaf + 1) % 2]
        for j in range(tiles):
            fill(j, *now)
            if leaf + 1 < leaves:
                find(leaf + 1, j, *later)
        multiply(leaf, now[3])


def exchange_kernel(
    inner,
    outer,
    coords_hbm,
    noise_hbm,
    order_hbm,
    probes_hbm,
    factors_hbm,
    dense_ref,
    sib_ref,
    left_ref,
    coords,
    noise,
    order,
    probes,
    right,
    beside,
    even,
    odd,
    counts,
    slots,
    table,
    ask,
    asked,
    give,
    given,
    part,
    parts,
    outer_part,
    outer_parts,
    total,
    totals,
    pairs,
    back,
    backs,
    outer_back,
    outer_backs,
    load_sem,
    send_sem,
    recv_sem,
):
    gx, gy = lax.axis_index("gx"), lax.axis_index("gy")
    points = order.shape[1]
    slot = points // inner
    levels = right.shape[0]
    far = levels - 2
    inner_bits = inner.bit_length() - 1
    outer_bits = outer.bit_length() - 1
    share = PROBES // inner
    owner_share = PROBES // OWNERS
    half = inner_bits * RANK
    owner = gy < OWNERS

    barrier = pltpu.get_barrier_semaphore()
    for axis, own, size in (("gy", gy, inner), ("gx", gx, outer)):

        @pl.loop(1, size)
        def _(j):
            pl.semaphore_signal(barrier, inc=1, device_id={axis: lax.rem(own + j, size)})

    loads = [
        pltpu.make_async_copy(source, target, load_sem.at[i])
        for i, (source, target) in enumerate(
            (
                (order_hbm, order),
                (coords_hbm, coords),
                (noise_hbm, noise),
                (probes_hbm, probes),
                (factors_hbm.at[2:, 1], right.at[2:]),
                (factors_hbm.at[:2, 1], right.at[:2]),
                (factors_hbm.at[:2, 0], beside),
                (factors_hbm.at[2:, 0], left_ref),
            )
        )
    ]
    for load in loads[:5]:
        load.start()

    def send(step, source, target, axis, peer):
        pltpu.make_async_remote_copy(
            src_ref=source,
            dst_ref=target,
            send_sem=send_sem.at[step],
            recv_sem=recv_sem.at[step],
            device_id={axis: peer},
        ).start()

    def wait_all(sems, step, ref, first, count):
        whole = ref.at[pl.ds(first, count)]
        pltpu.make_async_copy(whole, whole, sems.at[step]).wait()

    loads[0].wait()
    wanted = order[...]
    source = ((wanted >> (points.bit_length() - 1)) - gy) & (inner - 1)
    local_index = wanted & (points - 1)
    kind = lax.broadcasted_iota(jnp.int32, (inner, TILE), 0)
    chunks = points // TILE
    for k in range(chunks):
        counts[k * inner : (k + 1) * inner, :] = (
            kind == source[:, k * TILE : (k + 1) * TILE]
        ).astype(jnp.bfloat16)
    before = lax.broadcasted_iota(jnp.int32, (TILE, 2 * TILE), 0)
    column = lax.broadcasted_iota(jnp.int32, (TILE, 2 * TILE), 1)
    ones = ((before < column) | (column >= TILE)).astype(jnp.bfloat16)
    ahead = dot(counts[...], ones)
    offset = jnp.zeros((inner, TILE), jnp.float32)
    for k in range(chunks):
        rows = ahead[k * inner : (k + 1) * inner]
        own_source = source[:, k * TILE : (k + 1) * TILE]
        place = jnp.sum(
            jnp.where(kind == own_source, rows[:, :TILE] + offset, 0.0), axis=0, keepdims=True
        )
        slots[:, k * TILE : (k + 1) * TILE] = own_source * slot + place.astype(jnp.int32)
        offset = offset + rows[:, TILE:]

    place = slots[...]
    upper = lax.broadcasted_iota(jnp.int32, (points // LANES, points), 0) == (place >> 7)
    lower = lax.broadcasted_iota(jnp.int32, (LANES, points), 0) == (place & (LANES - 1))
    low_part = (local_index & 63).astype(jnp.float32)
    high_part = (local_index >> 6).astype(jnp.float32)
    marked = jnp.concatenate(
        [jnp.where(upper, low_part, 0.0), jnp.where(upper, high_part, 0.0)], axis=0
    ).astype(jnp.bfloat16)
    lists = dot(marked, lower.astype(jnp.bfloat16), NT)
    lists = (lists[: points // LANES] + 64.0 * lists[points // LANES :]).astype(jnp.int32)
    for j in range(inner):
        ask[j] = lists[2 * j : 2 * j + 2]

    loads[3].wait()
    loads[4].wait()
    vectors = probes[...]
    coeff = dot(vectors, right[2:].reshape(far * RANK, points), NT)
    for k in range(OWNERS):
        outer_part[k] = coeff[k * owner_share : (k + 1) * owner_share, half:]
    for k in range(inner):
        part[k] = coeff[k * share : (k + 1) * share, :half]
    parts[pl.ds(gy, 1)] = part[pl.ds(gy, 1)]

    pl.semaphore_wait(barrier, inner + outer - 2)

    @pl.loop(0, inner - 1, unroll=True)
    def _(step):
        j = far_first(step, inner)
        send(0, ask.at[j], asked.at[j], "gy", lax.rem(gy + j, inner))

    @pl.loop(0, OWNERS)
    def _(k):
        @pl.when(k != gy)
        def _():
            send(3, outer_part.at[k], outer_parts.at[gy], "gy", k)

    @pl.when(owner)
    def _():
        outer_parts[pl.ds(gy, 1)] = outer_part[pl.ds(gy, 1)]

    @pl.loop(0, inner - 1)
    def _(step):
        peer = lax.rem(gy + far_first(step, inner), inner)
        send(2, part.at[peer], parts.at[gy], "gy", peer)

    for load in loads[5:]:
        load.start()
    loads[1].wait()
    loads[2].wait()
    values = jnp.concatenate([coords[...], noise[...]], axis=0)
    vectors_own = [
        jnp.concatenate(
            [values[:, c * LANES : (c + 1) * LANES] for c in (2 * r, 2 * r + 1)], axis=0
        )
        for r in range(points // TILE)
    ]
    for r in range(points // TILE):
        table[r] = vectors_own[r]

    given[0] = look_up(vectors_own, ask[0, 0:1], ask[0, 1:2])

    loads[5].wait()
    loads[6].wait()
    near = [
        dot(
            vectors[:, a * LEAF : (a + 1) * LEAF],
            right[:2, :, a * LEAF : (a + 1) * LEAF].reshape(2 * RANK, LEAF),
            NT,
        )
        for a in range(points // LEAF)
    ]
    level = lax.broadcasted_iota(jnp.int32, (PROBES, 2 * RANK), 1) < RANK
    for a in range(points // LEAF):
        other = 2 * (1 - a // 2)
        sibling = jnp.where(level, near[a ^ 1], near[other] + near[other + 1])
        dense_ref[:, a * LEAF : (a + 1) * LEAF] = dot(
            sibling.astype(jnp.bfloat16),
            beside[:, :, a * LEAF : (a + 1) * LEAF].reshape(2 * RANK, LEAF),
        )

    @pl.when(owner)
    def _():
        wait_all(recv_sem, 3, outer_parts, 0, inner - 1)
        sums = [outer_parts[e] for e in range(inner)]
        while len(sums) > 1:
            sums = [sums[2 * g] + sums[2 * g + 1] for g in range(len(sums) // 2)]
        total[...] = sums[0]
        totals[pl.ds(gx, 1)] = sums[0][None]

        @pl.loop(1, outer, unroll=True)
        def _(j):
            send(4, total, totals.at[gx], "gx", lax.rem(gx + j, outer))

    wait_all(recv_sem, 0, asked, 1, inner - 1)

    @pl.loop(0, inner - 1)
    def _(step):
        j = far_first(step, inner)
        own_table = [table[r] for r in range(points // TILE)]
        lists = asked[j]
        give[j] = look_up(own_table, lists[0:1], lists[1:2])
        send(1, give.at[j], given.at[j], "gy", lax.rem(gy - j + inner, inner))

    wait_all(recv_sem, 2, parts, 0, inner - 1)
    lane = lax.broadcasted_iota(jnp.int32, (share, half), 1)
    sums = [[parts[e] for e in range(inner)]]
    for step in range(inner_bits - 1):
        last = sums[-1]
        sums.append([last[2 * g] + last[2 * g + 1] for g in range(len(last) // 2)])
    for d in range(inner):
        picked = sums[inner_bits - 1][(d >> (inner_bits - 1)) ^ 1]
        for h in reversed(range(inner_bits - 1)):
            picked = jnp.where(lane < (h + 1) * RANK, sums[h][(d >> h) ^ 1], picked)
        back[d] = picked
    backs[pl.ds(gy, 1)] = back[pl.ds(gy, 1)]

    @pl.loop(0, inner - 1)
    def _(step):
        peer = lax.rem(gy + far_first(step, inner), inner)
        send(5, back.at[peer], backs.at[gy], "gy", peer)

    @pl.when(owner)
    def _():
        wait_all(recv_sem, 4, totals, 0, outer - 1)
        width = outer_bits * RANK
        lane = lax.broadcasted_iota(jnp.int32, (owner_share, width), 1)
        base = 0
        sums = [totals[e] for e in range(outer)]
        picked = None
        for h in range(outer_bits):
            for g, value in enumerate(sums):
                pairs[base + g] = value
            group = gx // 2**h
            sibling = pairs[base + group + 1 - 2 * (group % 2)]
            picked = sibling if picked is None else jnp.where(lane < h * RANK, picked, sibling)
            base += len(sums)
            sums = [sums[2 * g] + sums[2 * g + 1] for g in range(len(sums) // 2)]
        outer_back[...] = picked
        outer_backs[pl.ds(gy, 1)] = picked[None]

        @pl.loop(1, inner, unroll=True)
        def _(j):
            send(6, outer_back, outer_backs.at[gy], "gy", lax.rem(gy + j, inner))

    wait_all(recv_sem, 1, given, 1, inner - 1)
    leaf_products(given, slots, probes, even, odd, dense_ref)

    wait_all(recv_sem, 5, backs, 0, inner - 1)

    @pl.when(owner)
    def _():
        wait_all(recv_sem, 6, outer_backs, 0, OWNERS - 1)

    @pl.when(jnp.logical_not(owner))
    def _():
        wait_all(recv_sem, 6, outer_backs, 0, OWNERS)

    sib_ref[...] = jnp.concatenate(
        [
            jnp.concatenate([backs[k] for k in range(inner)], axis=0),
            jnp.concatenate([outer_backs[k] for k in range(OWNERS)], axis=0),
        ],
        axis=1,
    ).astype(jnp.bfloat16)

    loads[7].wait()
    wait_all(send_sem, 0, ask, 1, inner - 1)
    wait_all(send_sem, 1, give, 1, inner - 1)
    wait_all(send_sem, 2, part, 0, inner - 1)
    wait_all(send_sem, 5, back, 0, inner - 1)

    @pl.when(owner)
    def _():
        wait_all(send_sem, 3, outer_part, 0, OWNERS - 1)
        wait_all(send_sem, 4, totals, 0, outer - 1)
        wait_all(send_sem, 6, outer_parts, 0, inner - 1)

    @pl.when(jnp.logical_not(owner))
    def _():
        wait_all(send_sem, 3, outer_part, 0, OWNERS)


def exchange(inner, outer, coords, noise, order, probes, factors):
    points = probes.shape[1]
    levels = factors.shape[0]
    far = levels - 2
    share = PROBES // inner
    owner_share = PROBES // OWNERS
    inner_bits = inner.bit_length() - 1
    outer_bits = outer.bit_length() - 1
    wide = far * RANK
    f32, bf16, i32 = jnp.float32, jnp.bfloat16, jnp.int32
    hbm = pl.BlockSpec(memory_space=pltpu.HBM)
    leaf_set = (
        pltpu.VMEM((1, LEAF), f32),
        pltpu.VMEM((LEAF, 32), bf16),
        pltpu.VMEM((32, LEAF), bf16),
        pltpu.VMEM((LEAF, LEAF), bf16),
    )
    vmem = pl.BlockSpec(memory_space=pltpu.VMEM)
    return pl.pallas_call(
        functools.partial(exchange_kernel, inner, outer),
        out_shape=(
            jax.ShapeDtypeStruct((PROBES, points), f32),
            jax.ShapeDtypeStruct((PROBES, wide), bf16),
            jax.ShapeDtypeStruct((far, RANK, points), bf16),
        ),
        in_specs=[hbm] * 5,
        out_specs=(vmem, vmem, vmem),
        scratch_shapes=[
            pltpu.VMEM((3, points), f32),
            pltpu.VMEM((1, points), f32),
            pltpu.VMEM((1, points), i32),
            pltpu.VMEM((PROBES, points), bf16),
            pltpu.VMEM((levels, RANK, points), bf16),
            pltpu.VMEM((2, RANK, points), bf16),
            leaf_set,
            leaf_set,
            pltpu.VMEM((inner * points // TILE, TILE), bf16),
            pltpu.VMEM((1, points), i32),
            pltpu.VMEM((points // TILE, 8, LANES), f32),
            pltpu.VMEM((inner, 2, LANES), i32),
            pltpu.VMEM((inner, 2, LANES), i32),
            pltpu.VMEM((inner, 8, LANES), f32),
            pltpu.VMEM((inner, 8, LANES), f32),
            pltpu.VMEM((inner, share, inner_bits * RANK), f32),
            pltpu.VMEM((inner, share, inner_bits * RANK), f32),
            pltpu.VMEM((OWNERS, owner_share, outer_bits * RANK), f32),
            pltpu.VMEM((inner, owner_share, outer_bits * RANK), f32),
            pltpu.VMEM((owner_share, outer_bits * RANK), f32),
            pltpu.VMEM((outer, owner_share, outer_bits * RANK), f32),
            pltpu.VMEM((2 * outer, owner_share, outer_bits * RANK), f32),
            pltpu.VMEM((inner, share, inner_bits * RANK), f32),
            pltpu.VMEM((inner, share, inner_bits * RANK), f32),
            pltpu.VMEM((owner_share, outer_bits * RANK), f32),
            pltpu.VMEM((OWNERS, owner_share, outer_bits * RANK), f32),
            pltpu.SemaphoreType.DMA((8,)),
            pltpu.SemaphoreType.DMA((7,)),
            pltpu.SemaphoreType.DMA((7,)),
        ],
        compiler_params=pltpu.CompilerParams(
            collective_id=0, has_side_effects=True, vmem_limit_bytes=40 * 2**20
        ),
    )(
        *(
            pltpu.with_memory_space_constraint(array, pltpu.HBM)
            for array in (coords, noise.reshape(1, points), order, probes, factors)
        )
    )


def expand_kernel(dense, sib, left, out_hbm, result, sems):
    points = dense.shape[1]
    width = result.shape[2]
    writes = []
    for c in range(points // width):
        columns = slice(c * width, (c + 1) * width)
        result[c] = dense[:, columns] + dot(
            sib[...], left[:, :, columns].reshape(sib.shape[1], width)
        )
        writes.append(
            pltpu.make_async_copy(result.at[c], out_hbm.at[:, columns], sems.at[c])
        )
        writes[-1].start()
    for write in writes:
        write.wait()


def expand(dense, sib, left):
    points = dense.shape[1]
    width = 512
    vmem = pl.BlockSpec(memory_space=pltpu.VMEM)
    return pl.pallas_call(
        expand_kernel,
        out_shape=jax.ShapeDtypeStruct((PROBES, points), jnp.float32),
        in_specs=[vmem] * 3,
        out_specs=pl.BlockSpec(memory_space=pltpu.HBM),
        scratch_shapes=[
            pltpu.VMEM((points // width, PROBES, width), jnp.float32),
            pltpu.SemaphoreType.DMA((points // width,)),
        ],
        compiler_params=pltpu.CompilerParams(vmem_limit_bytes=16 * 2**20),
    )(dense, sib, left)


def solution(mesh):
    inner, outer = mesh.shape["gy"], mesh.shape["gx"]

    def local(coords, noise, order, probes, factors):
        return expand(*exchange(inner, outer, coords, noise, order, probes, factors))

    return jax.shard_map(
        local,
        mesh=mesh,
        in_specs=(
            P(None, ("gx", "gy")),
            P(("gx", "gy")),
            P("gx", "gy"),
            P(None, ("gx", "gy")),
            P(None, None, None, ("gx", "gy")),
        ),
        out_specs=P(None, ("gx", "gy")),
        check_vma=False,
    )
```

```python
import functools

import jax
import jax.numpy as jnp
from jax import lax
from jax.experimental import pallas as pl
from jax.experimental.pallas import tpu as pltpu
from jax.sharding import PartitionSpec as P

LEAF = 1024
RANK = 32
PROBES = 64
LANES = 128
TILE = 256
OWNERS = 8
NT = (((1,), (1,)), ((), ()))
SQRT_THREE = 1.7320508075688772
LOG2_E = 1.4426950408889634


def dot(a, b, dims=(((1,), (0,)), ((), ()))):
    return lax.dot_general(a, b, dims, preferred_element_type=jnp.float32)


def look_up(table, first, second):
    shape = (8, LANES)
    found = []
    for picks in (first, second):
        picks = jnp.broadcast_to(picks, shape)
        lane = picks & (LANES - 1)
        out = [
            jnp.take_along_axis(vector, lane, axis=1, mode="promise_in_bounds") for vector in table
        ]
        bit = 8
        while len(out) > 1:
            odd = ((picks >> bit) & 1) == 1
            out = [jnp.where(odd, out[g + 1], out[g]) for g in range(0, len(out), 2)]
            bit += 1
        found.append((out[0], ((picks >> 7) & 1) == 0))
    row = lax.broadcasted_iota(jnp.int32, shape, 0)
    (one, one_low), (two, two_low) = found
    return jnp.where(
        row < 4,
        jnp.where(one_low, one, pltpu.roll(one, 4, 0)),
        jnp.where(two_low, pltpu.roll(two, 4, 0), two),
    )


def split_three(x):
    one = x.astype(jnp.bfloat16)
    rest = x - one.astype(jnp.float32)
    two = rest.astype(jnp.bfloat16)
    three = (rest - two.astype(jnp.float32)).astype(jnp.bfloat16)
    return one.astype(jnp.float32), two.astype(jnp.float32), three.astype(jnp.float32)


def far_first(step, size):
    odd = lax.rem(step, 2)
    return size // 2 + odd * ((step + 1) // 2) - (1 - odd) * (step // 2)


def leaf_features(values):
    spots = (values[0:3] - 4.0) * SQRT_THREE
    norm = spots * spots
    norm = norm[0:1] + norm[1:2] + norm[2:3]
    a, b, c = split_three(spots)
    n1, n2, n3 = split_three(norm)
    unit = jnp.ones_like(norm)
    pad = jnp.zeros((8, norm.shape[1]), jnp.float32)
    one = jnp.concatenate([a, a, b, a, c, b, n1, n2, n3, unit, unit, unit, pad], axis=0)
    two = jnp.concatenate(
        [-2.0 * v for v in (a, b, a, c, a, b)] + [unit, unit, unit, n1, n2, n3, pad], axis=0
    )
    return one.astype(jnp.bfloat16), two.astype(jnp.bfloat16)


def matern(square):
    scaled = square * lax.rsqrt(jnp.maximum(square, 1e-3))
    return (1.0 + scaled) * jnp.exp2(scaled * -LOG2_E)


def leaf_products(given, slots, probes, even, odd, out_ref):
    points = slots.shape[1]
    half = TILE // 2
    tiles = LEAF // TILE

    def multiply(leaf, j, block_ref):
        start = leaf * LEAF
        first, last = j * TILE, (j + 1) * TILE
        columns = slice(start + first, start + last)
        total = out_ref[:, columns] + dot(
            probes[:, start : start + last], block_ref[:last, first:last]
        )
        if j < tiles - 1:
            total = total + dot(
                probes[:, start + last : start + LEAF], block_ref[first:last, last:], NT
            )
        out_ref[:, columns] = total

    def multiply_now(leaf, j, block_ref):
        start = leaf * LEAF
        first, last = j * TILE, (j + 1) * TILE
        columns = slice(start + first, start + last)
        out_ref[:, columns] += dot(probes[:, start : start + last], block_ref[:last, first:last])
        for i in range(j):
            before = slice(start + i * TILE, start + (i + 1) * TILE)
            out_ref[:, before] += dot(
                probes[:, columns], block_ref[i * TILE : (i + 1) * TILE, first:last], NT
            )

    def find(leaf, j, noise_ref, one_ref, two_ref, block_ref):
        at = leaf * LEAF + j * TILE
        found = look_up(
            [given[r] for r in range(given.shape[0])],
            slots[:, pl.ds(pl.multiple_of(at, LANES), LANES)],
            slots[:, pl.ds(pl.multiple_of(at + LANES, LANES), LANES)],
        )
        columns = slice(j * TILE, (j + 1) * TILE)
        values = jnp.concatenate([found[0:4], found[4:8]], axis=1)
        one, two = leaf_features(values)
        one_ref[columns, :] = one.T
        two_ref[:, columns] = two
        noise_ref[:, columns] = 1.0 + values[3:4]

    def fill(j, noise_ref, one_ref, two_ref, block_ref):
        first, middle, last = j * TILE, j * TILE + half, (j + 1) * TILE
        eye = lax.broadcasted_iota(jnp.int32, (half, half), 0) == lax.broadcasted_iota(
            jnp.int32, (half, half), 1
        )
        if j:
            block_ref[:first, first:last] = matern(
                dot(one_ref[:first], two_ref[:, first:last])
            ).astype(jnp.bfloat16)
        upper = matern(dot(one_ref[first:middle], two_ref[:, first:last]))
        side = upper[:, half:].astype(jnp.bfloat16)
        block_ref[first:middle, first:middle] = jnp.where(
            eye, noise_ref[:, first:middle], upper[:, :half]
        ).astype(jnp.bfloat16)
        block_ref[first:middle, middle:last] = side
        block_ref[middle:last, first:middle] = side.T
        block_ref[middle:last, middle:last] = jnp.where(
            eye,
            noise_ref[:, middle:last],
            matern(dot(one_ref[middle:last], two_ref[:, middle:last])),
        ).astype(jnp.bfloat16)

    leaves = points // LEAF

    sets = (even, odd)
    for j in range(tiles):
        find(0, j, *even)
    for leaf in range(leaves):
        now, other = sets[leaf % 2], sets[(leaf + 1) % 2]
        for j in range(tiles):
            fill(j, *now)
            if leaf:
                multiply(leaf - 1, j, other[3])
            if leaf + 1 < leaves:
                find(leaf + 1, j, *other)
    for j in range(tiles):
        multiply(leaves - 1, j, sets[(leaves - 1) % 2][3])


def exchange_kernel(
    inner,
    outer,
    coords_hbm,
    noise_hbm,
    order_hbm,
    probes_hbm,
    factors_hbm,
    dense_ref,
    sib_ref,
    left_ref,
    coords,
    noise,
    order,
    probes,
    right,
    beside,
    even,
    odd,
    counts,
    slots,
    table,
    ask,
    asked,
    give,
    given,
    part,
    parts,
    outer_part,
    outer_parts,
    total,
    totals,
    pairs,
    back,
    backs,
    outer_back,
    outer_backs,
    ready,
    load_sem,
    send_sem,
    recv_sem,
):
    gx, gy = lax.axis_index("gx"), lax.axis_index("gy")
    points = order.shape[1]
    slot = points // inner
    levels = right.shape[0]
    far = levels - 2
    inner_bits = inner.bit_length() - 1
    outer_bits = outer.bit_length() - 1
    share = PROBES // OWNERS
    late = inner - OWNERS
    half = inner_bits * RANK
    owner = gy < OWNERS

    outer_first = levels - outer_bits
    loads = [
        pltpu.make_async_copy(source, target, load_sem.at[i])
        for i, (source, target) in enumerate(
            (
                (probes_hbm, probes),
                (factors_hbm.at[outer_first:, 1], right.at[outer_first:]),
                (order_hbm, order),
                (coords_hbm, coords),
                (noise_hbm, noise),
                (factors_hbm.at[2:outer_first, 1], right.at[2:outer_first]),
                (factors_hbm.at[:2, 1], right.at[:2]),
                (factors_hbm.at[:2, 0], beside),
                (factors_hbm.at[2:, 0], left_ref),
            )
        )
    ]
    for load in loads[:6]:
        load.start()

    barrier = pltpu.get_barrier_semaphore()

    @pl.when(owner)
    def _():
        @pl.loop(0, inner - 1)
        def _(step):
            peer = lax.rem(gy + far_first(step, inner), inner)
            pl.semaphore_signal(barrier, inc=1, device_id={"gy": peer})

        @pl.loop(0, outer - 1)
        def _(step):
            peer = lax.rem(gx + far_first(step, outer), outer)
            pl.semaphore_signal(barrier, inc=1, device_id={"gx": peer})

    @pl.when(jnp.logical_not(owner))
    def _():
        pl.semaphore_wait(barrier, OWNERS)

        @pl.loop(0, OWNERS)
        def _(k):
            pl.semaphore_signal(ready, inc=1, device_id={"gy": k})

    def send(step, source, target, axis, peer, arrival=None):
        pltpu.make_async_remote_copy(
            src_ref=source,
            dst_ref=target,
            send_sem=send_sem.at[step],
            recv_sem=recv_sem.at[step if arrival is None else arrival],
            device_id={axis: peer},
        ).start()

    def others(first, last, body):
        @pl.loop(first, last)
        def _(k):
            pl.when(k != gy)(lambda: body(k))

    def request(arrival):
        def to(k):
            j = lax.rem(k - gy + inner, inner)
            send(0, ask.at[j], asked.at[j], "gy", k, arrival)

        return to

    def give_part(k):
        send(3, outer_part.at[k], outer_parts.at[gy], "gy", k)

    def give_inner_part(k):
        send(2, part.at[k], parts.at[gy], "gy", k)

    def answer(j):
        own_table = [table[r] for r in range(points // TILE)]
        lists = asked[j]
        give[j] = look_up(own_table, lists[0:1], lists[1:2])
        send(1, give.at[j], given.at[j], "gy", lax.rem(gy - j + inner, inner))

    def wait_all(sems, step, ref, first, count):
        whole = ref.at[pl.ds(first, count)]
        pltpu.make_async_copy(whole, whole, sems.at[step]).wait()

    loads[0].wait()
    loads[1].wait()
    vectors = probes[...]
    coeff = dot(vectors, right[outer_first:].reshape(outer_bits * RANK, points), NT)
    for k in range(OWNERS):
        outer_part[k] = coeff[k * share : (k + 1) * share]

    @pl.when(jnp.logical_not(owner))
    def _():
        others(0, OWNERS, give_part)

    loads[2].wait()
    wanted = order[...]
    source = ((wanted >> (points.bit_length() - 1)) - gy) & (inner - 1)
    local_index = wanted & (points - 1)
    kind = lax.broadcasted_iota(jnp.int32, (inner, TILE), 0)
    chunks = points // TILE
    for k in range(chunks):
        counts[k * inner : (k + 1) * inner, :] = (
            kind == source[:, k * TILE : (k + 1) * TILE]
        ).astype(jnp.bfloat16)
    before = lax.broadcasted_iota(jnp.int32, (TILE, 2 * TILE), 0)
    column = lax.broadcasted_iota(jnp.int32, (TILE, 2 * TILE), 1)
    ones = ((before < column) | (column >= TILE)).astype(jnp.bfloat16)
    ahead = dot(counts[...], ones)
    offset = jnp.zeros((inner, TILE), jnp.float32)
    for k in range(chunks):
        rows = ahead[k * inner : (k + 1) * inner]
        own_source = source[:, k * TILE : (k + 1) * TILE]
        place = jnp.sum(
            jnp.where(kind == own_source, rows[:, :TILE] + offset, 0.0), axis=0, keepdims=True
        )
        slots[:, k * TILE : (k + 1) * TILE] = own_source * slot + place.astype(jnp.int32)
        offset = offset + rows[:, TILE:]

    place = slots[...]
    upper = lax.broadcasted_iota(jnp.int32, (points // LANES, points), 0) == (place >> 7)
    lower = lax.broadcasted_iota(jnp.int32, (LANES, points), 0) == (place & (LANES - 1))
    low_part = (local_index & 63).astype(jnp.float32)
    high_part = (local_index >> 6).astype(jnp.float32)
    marked = jnp.concatenate(
        [jnp.where(upper, low_part, 0.0), jnp.where(upper, high_part, 0.0)], axis=0
    ).astype(jnp.bfloat16)
    lists = dot(marked, lower.astype(jnp.bfloat16), NT)
    lists = (lists[: points // LANES] + 64.0 * lists[points // LANES :]).astype(jnp.int32)
    for j in range(inner):
        ask[j] = lists[2 * j : 2 * j + 2]

    @pl.when(jnp.logical_not(owner))
    def _():
        others(0, OWNERS, request(7))

    loads[5].wait()
    coeff = dot(vectors, right[2:outer_first].reshape(inner_bits * RANK, points), NT)
    for k in range(OWNERS):
        part[k] = coeff[k * share : (k + 1) * share]

    @pl.when(jnp.logical_not(owner))
    def _():
        others(0, OWNERS, give_inner_part)

    for load in loads[6:]:
        load.start()

    loads[3].wait()
    loads[4].wait()
    values = jnp.concatenate([coords[...], noise[...]], axis=0)
    vectors_own = [
        jnp.concatenate(
            [values[:, c * LANES : (c + 1) * LANES] for c in (2 * r, 2 * r + 1)], axis=0
        )
        for r in range(points // TILE)
    ]
    for r in range(points // TILE):
        table[r] = vectors_own[r]

    @pl.when(owner)
    def _():
        parts[pl.ds(gy, 1)] = part[pl.ds(gy, 1)]
        outer_parts[pl.ds(gy, 1)] = outer_part[pl.ds(gy, 1)]
        pl.semaphore_wait(barrier, OWNERS - 1 + outer - 1)
        others(0, OWNERS, give_part)
        others(0, OWNERS, request(0))
        pl.semaphore_wait(ready, late)
        others(OWNERS, inner, request(0))
        others(0, OWNERS, give_inner_part)

    given[0] = look_up(vectors_own, ask[0, 0:1], ask[0, 1:2])

    loads[6].wait()
    loads[7].wait()
    near = [
        dot(
            vectors[:, a * LEAF : (a + 1) * LEAF],
            right[:2, :, a * LEAF : (a + 1) * LEAF].reshape(2 * RANK, LEAF),
            NT,
        )
        for a in range(points // LEAF)
    ]
    level = lax.broadcasted_iota(jnp.int32, (PROBES, 2 * RANK), 1) < RANK
    for a in range(points // LEAF):
        other = 2 * (1 - a // 2)
        sibling = jnp.where(level, near[a ^ 1], near[other] + near[other + 1])
        dense_ref[:, a * LEAF : (a + 1) * LEAF] = dot(
            sibling.astype(jnp.bfloat16),
            beside[:, :, a * LEAF : (a + 1) * LEAF].reshape(2 * RANK, LEAF),
        )

    @pl.when(owner)
    def _():
        wait_all(recv_sem, 3, outer_parts, 0, inner - 1)
        sums = [outer_parts[e] for e in range(inner)]
        while len(sums) > 1:
            sums = [sums[2 * g] + sums[2 * g + 1] for g in range(len(sums) // 2)]
        total[...] = sums[0]
        totals[pl.ds(gx, 1)] = sums[0][None]

        @pl.loop(0, outer - 1, unroll=True)
        def _(step):
            peer = lax.rem(gx + far_first(step, outer), outer)
            send(4, total, totals.at[gx], "gx", peer)

    @pl.when(owner)
    def _():
        wait_all(recv_sem, 7, asked, 0, late)
        wait_all(recv_sem, 0, asked, 0, OWNERS - 1)

        @pl.loop(0, inner - 1)
        def _(step):
            answer(far_first(step, inner))

    @pl.when(jnp.logical_not(owner))
    def _():
        wait_all(recv_sem, 0, asked, 0, OWNERS)
        others(0, OWNERS, lambda k: answer(lax.rem(gy - k + inner, inner)))
        others(OWNERS, inner, request(7))
        wait_all(recv_sem, 7, asked, 0, late - 1)
        others(OWNERS, inner, lambda k: answer(lax.rem(gy - k + inner, inner)))

    @pl.when(owner)
    def _():
        wait_all(recv_sem, 2, parts, 0, inner - 1)
        lane = lax.broadcasted_iota(jnp.int32, (share, half), 1)
        sums = [[parts[e] for e in range(inner)]]
        for step in range(inner_bits - 1):
            last = sums[-1]
            sums.append([last[2 * g] + last[2 * g + 1] for g in range(len(last) // 2)])
        for d in range(inner):
            picked = sums[inner_bits - 1][(d >> (inner_bits - 1)) ^ 1]
            for h in reversed(range(inner_bits - 1)):
                picked = jnp.where(lane < (h + 1) * RANK, sums[h][(d >> h) ^ 1], picked)
            back[d] = picked
        backs[pl.ds(gy, 1)] = back[pl.ds(gy, 1)]
        others(0, inner, lambda k: send(5, back.at[k], backs.at[gy], "gy", k))

    @pl.when(owner)
    def _():
        wait_all(recv_sem, 4, totals, 0, outer - 1)
        width = outer_bits * RANK
        lane = lax.broadcasted_iota(jnp.int32, (share, width), 1)
        base = 0
        sums = [totals[e] for e in range(outer)]
        picked = None
        for h in range(outer_bits):
            for g, value in enumerate(sums):
                pairs[base + g] = value
            group = gx // 2**h
            sibling = pairs[base + group + 1 - 2 * (group % 2)]
            picked = sibling if picked is None else jnp.where(lane < h * RANK, picked, sibling)
            base += len(sums)
            sums = [sums[2 * g] + sums[2 * g + 1] for g in range(len(sums) // 2)]
        outer_back[...] = picked
        outer_backs[pl.ds(gy, 1)] = picked[None]

        others(0, inner, lambda k: send(6, outer_back, outer_backs.at[gy], "gy", k))

    wait_all(recv_sem, 1, given, 1, inner - 1)
    leaf_products(given, slots, probes, even, odd, dense_ref)

    @pl.when(owner)
    def _():
        wait_all(recv_sem, 5, backs, 0, OWNERS - 1)
        wait_all(recv_sem, 6, outer_backs, 0, OWNERS - 1)

    @pl.when(jnp.logical_not(owner))
    def _():
        wait_all(recv_sem, 5, backs, 0, OWNERS)
        wait_all(recv_sem, 6, outer_backs, 0, OWNERS)

    for k in range(OWNERS):
        sib_ref[k * share : (k + 1) * share, :] = jnp.concatenate(
            [backs[k], outer_backs[k]], axis=1
        )

    loads[8].wait()
    wait_all(send_sem, 0, ask, 1, inner - 1)
    wait_all(send_sem, 1, give, 1, inner - 1)

    @pl.when(owner)
    def _():
        wait_all(send_sem, 2, part, 0, OWNERS - 1)
        wait_all(send_sem, 3, outer_part, 0, OWNERS - 1)
        wait_all(send_sem, 4, totals, 0, outer - 1)
        wait_all(send_sem, 5, back, 0, inner - 1)
        wait_all(send_sem, 6, outer_parts, 0, inner - 1)

    @pl.when(jnp.logical_not(owner))
    def _():
        wait_all(send_sem, 2, part, 0, OWNERS)
        wait_all(send_sem, 3, outer_part, 0, OWNERS)


def exchange(inner, outer, coords, noise, order, probes, factors):
    points = probes.shape[1]
    levels = factors.shape[0]
    far = levels - 2
    share = PROBES // OWNERS
    inner_bits = inner.bit_length() - 1
    outer_bits = outer.bit_length() - 1
    wide = far * RANK
    f32, bf16, i32 = jnp.float32, jnp.bfloat16, jnp.int32
    hbm = pl.BlockSpec(memory_space=pltpu.HBM)
    leaf_set = (
        pltpu.VMEM((1, LEAF), f32),
        pltpu.VMEM((LEAF, 32), bf16),
        pltpu.VMEM((32, LEAF), bf16),
        pltpu.VMEM((LEAF, LEAF), bf16),
    )
    vmem = pl.BlockSpec(memory_space=pltpu.VMEM)
    return pl.pallas_call(
        functools.partial(exchange_kernel, inner, outer),
        out_shape=(
            jax.ShapeDtypeStruct((PROBES, points), f32),
            jax.ShapeDtypeStruct((PROBES, wide), f32),
            jax.ShapeDtypeStruct((far, RANK, points), bf16),
        ),
        in_specs=[hbm] * 5,
        out_specs=(vmem, vmem, vmem),
        scratch_shapes=[
            pltpu.VMEM((3, points), f32),
            pltpu.VMEM((1, points), f32),
            pltpu.VMEM((1, points), i32),
            pltpu.VMEM((PROBES, points), bf16),
            pltpu.VMEM((levels, RANK, points), bf16),
            pltpu.VMEM((2, RANK, points), bf16),
            leaf_set,
            leaf_set,
            pltpu.VMEM((inner * points // TILE, TILE), bf16),
            pltpu.VMEM((1, points), i32),
            pltpu.VMEM((points // TILE, 8, LANES), f32),
            pltpu.VMEM((inner, 2, LANES), i32),
            pltpu.VMEM((inner, 2, LANES), i32),
            pltpu.VMEM((inner, 8, LANES), f32),
            pltpu.VMEM((inner, 8, LANES), f32),
            pltpu.VMEM((OWNERS, share, inner_bits * RANK), f32),
            pltpu.VMEM((inner, share, inner_bits * RANK), f32),
            pltpu.VMEM((OWNERS, share, outer_bits * RANK), f32),
            pltpu.VMEM((inner, share, outer_bits * RANK), f32),
            pltpu.VMEM((share, outer_bits * RANK), f32),
            pltpu.VMEM((outer, share, outer_bits * RANK), f32),
            pltpu.VMEM((2 * outer, share, outer_bits * RANK), f32),
            pltpu.VMEM((inner, share, inner_bits * RANK), f32),
            pltpu.VMEM((OWNERS, share, inner_bits * RANK), f32),
            pltpu.VMEM((share, outer_bits * RANK), f32),
            pltpu.VMEM((OWNERS, share, outer_bits * RANK), f32),
            pltpu.SemaphoreType.REGULAR,
            pltpu.SemaphoreType.DMA((9,)),
            pltpu.SemaphoreType.DMA((7,)),
            pltpu.SemaphoreType.DMA((8,)),
        ],
        compiler_params=pltpu.CompilerParams(
            collective_id=0, has_side_effects=True, vmem_limit_bytes=40 * 2**20
        ),
    )(
        *(
            pltpu.with_memory_space_constraint(array, pltpu.HBM)
            for array in (coords, noise.reshape(1, points), order, probes, factors)
        )
    )


def expand_kernel(dense, sib, left, out_hbm, result, sems):
    points = dense.shape[1]
    width = result.shape[2]
    writes = []
    rounded = sib[...].astype(jnp.bfloat16)
    for c in range(points // width):
        columns = slice(c * width, (c + 1) * width)
        result[c] = dense[:, columns] + dot(
            rounded, left[:, :, columns].reshape(sib.shape[1], width)
        )
        writes.append(
            pltpu.make_async_copy(result.at[c], out_hbm.at[:, columns], sems.at[c])
        )
        writes[-1].start()
    for write in writes:
        write.wait()


def expand(dense, sib, left):
    points = dense.shape[1]
    width = 512
    vmem = pl.BlockSpec(memory_space=pltpu.VMEM)
    return pl.pallas_call(
        expand_kernel,
        out_shape=jax.ShapeDtypeStruct((PROBES, points), jnp.float32),
        in_specs=[vmem] * 3,
        out_specs=pl.BlockSpec(memory_space=pltpu.HBM),
        scratch_shapes=[
            pltpu.VMEM((points // width, PROBES, width), jnp.float32),
            pltpu.SemaphoreType.DMA((points // width,)),
        ],
        compiler_params=pltpu.CompilerParams(vmem_limit_bytes=16 * 2**20),
    )(dense, sib, left)


def solution(mesh):
    inner, outer = mesh.shape["gy"], mesh.shape["gx"]

    def local(coords, noise, order, probes, factors):
        return expand(*exchange(inner, outer, coords, noise, order, probes, factors))

    return jax.shard_map(
        local,
        mesh=mesh,
        in_specs=(
            P(None, ("gx", "gy")),
            P(("gx", "gy")),
            P("gx", "gy"),
            P(None, ("gx", "gy")),
            P(None, None, None, ("gx", "gy")),
        ),
        out_specs=P(None, ("gx", "gy")),
        check_vma=False,
    )
```

```python
import functools

import jax
import jax.numpy as jnp
from jax import lax
from jax.experimental import pallas as pl
from jax.experimental.pallas import tpu as pltpu
from jax.sharding import PartitionSpec as P

LEAF = 1024
RANK = 32
PROBES = 64
LANES = 128
TILE = 256
OWNERS = 8
NT = (((1,), (1,)), ((), ()))
SQRT_THREE = 1.7320508075688772
LOG2_E = 1.4426950408889634


def dot(a, b, dims=(((1,), (0,)), ((), ()))):
    return lax.dot_general(a, b, dims, preferred_element_type=jnp.float32)


def look_up(table, first, second):
    shape = (8, LANES)
    found = []
    for picks in (first, second):
        picks = jnp.broadcast_to(picks, shape)
        lane = picks & (LANES - 1)
        out = [
            jnp.take_along_axis(vector, lane, axis=1, mode="promise_in_bounds") for vector in table
        ]
        bit = 8
        while len(out) > 1:
            odd = ((picks >> bit) & 1) == 1
            out = [jnp.where(odd, out[g + 1], out[g]) for g in range(0, len(out), 2)]
            bit += 1
        found.append((out[0], ((picks >> 7) & 1) == 0))
    row = lax.broadcasted_iota(jnp.int32, shape, 0)
    (one, one_low), (two, two_low) = found
    return jnp.where(
        row < 4,
        jnp.where(one_low, one, pltpu.roll(one, 4, 0)),
        jnp.where(two_low, pltpu.roll(two, 4, 0), two),
    )


def split_three(x):
    one = x.astype(jnp.bfloat16)
    rest = x - one.astype(jnp.float32)
    two = rest.astype(jnp.bfloat16)
    three = (rest - two.astype(jnp.float32)).astype(jnp.bfloat16)
    return one.astype(jnp.float32), two.astype(jnp.float32), three.astype(jnp.float32)


def far_first(step, size):
    odd = lax.rem(step, 2)
    return size // 2 + odd * ((step + 1) // 2) - (1 - odd) * (step // 2)


def leaf_features(values):
    spots = (values[0:3] - 4.0) * SQRT_THREE
    norm = spots * spots
    norm = norm[0:1] + norm[1:2] + norm[2:3]
    a, b, c = split_three(spots)
    n1, n2, n3 = split_three(norm)
    unit = jnp.ones_like(norm)
    pad = jnp.zeros((8, norm.shape[1]), jnp.float32)
    one = jnp.concatenate([a, a, b, a, c, b, n1, n2, n3, unit, unit, unit, pad], axis=0)
    two = jnp.concatenate(
        [-2.0 * v for v in (a, b, a, c, a, b)] + [unit, unit, unit, n1, n2, n3, pad], axis=0
    )
    return one.astype(jnp.bfloat16), two.astype(jnp.bfloat16)


def matern(square):
    scaled = square * lax.rsqrt(jnp.maximum(square, 1e-3))
    return (1.0 + scaled) * jnp.exp2(scaled * -LOG2_E)


def leaf_products(given, slots, probes, even, odd, out_ref):
    points = slots.shape[1]
    half = TILE // 2
    tiles = LEAF // TILE

    def multiply(leaf, j, block_ref):
        start = leaf * LEAF
        first, last = j * TILE, (j + 1) * TILE
        columns = slice(start + first, start + last)
        total = out_ref[:, columns] + dot(
            probes[:, start : start + last], block_ref[:last, first:last]
        )
        if j < tiles - 1:
            total = total + dot(
                probes[:, start + last : start + LEAF], block_ref[first:last, last:], NT
            )
        out_ref[:, columns] = total

    def multiply_now(leaf, j, block_ref):
        start = leaf * LEAF
        first, last = j * TILE, (j + 1) * TILE
        columns = slice(start + first, start + last)
        out_ref[:, columns] += dot(probes[:, start : start + last], block_ref[:last, first:last])
        for i in range(j):
            before = slice(start + i * TILE, start + (i + 1) * TILE)
            out_ref[:, before] += dot(
                probes[:, columns], block_ref[i * TILE : (i + 1) * TILE, first:last], NT
            )

    def find(leaf, j, noise_ref, one_ref, two_ref, block_ref):
        at = leaf * LEAF + j * TILE
        found = look_up(
            [given[r] for r in range(given.shape[0])],
            slots[:, pl.ds(pl.multiple_of(at, LANES), LANES)],
            slots[:, pl.ds(pl.multiple_of(at + LANES, LANES), LANES)],
        )
        columns = slice(j * TILE, (j + 1) * TILE)
        values = jnp.concatenate([found[0:4], found[4:8]], axis=1)
        one, two = leaf_features(values)
        one_ref[columns, :] = one.T
        two_ref[:, columns] = two
        noise_ref[:, columns] = 1.0 + values[3:4]

    def fill(j, noise_ref, one_ref, two_ref, block_ref):
        first, middle, last = j * TILE, j * TILE + half, (j + 1) * TILE
        eye = lax.broadcasted_iota(jnp.int32, (half, half), 0) == lax.broadcasted_iota(
            jnp.int32, (half, half), 1
        )
        if j:
            block_ref[:first, first:last] = matern(
                dot(one_ref[:first], two_ref[:, first:last])
            ).astype(jnp.bfloat16)
        upper = matern(dot(one_ref[first:middle], two_ref[:, first:last]))
        side = upper[:, half:].astype(jnp.bfloat16)
        block_ref[first:middle, first:middle] = jnp.where(
            eye, noise_ref[:, first:middle], upper[:, :half]
        ).astype(jnp.bfloat16)
        block_ref[first:middle, middle:last] = side
        block_ref[middle:last, first:middle] = side.T
        block_ref[middle:last, middle:last] = jnp.where(
            eye,
            noise_ref[:, middle:last],
            matern(dot(one_ref[middle:last], two_ref[:, middle:last])),
        ).astype(jnp.bfloat16)

    leaves = points // LEAF

    sets = (even, odd)
    for j in range(tiles):
        find(0, j, *even)
    for leaf in range(leaves):
        now, other = sets[leaf % 2], sets[(leaf + 1) % 2]
        for j in range(tiles):
            fill(j, *now)
            if leaf:
                multiply(leaf - 1, j, other[3])
            if leaf + 1 < leaves:
                find(leaf + 1, j, *other)
    for j in range(tiles):
        multiply(leaves - 1, j, sets[(leaves - 1) % 2][3])


def exchange_kernel(
    inner,
    outer,
    coords_hbm,
    noise_hbm,
    order_hbm,
    probes_hbm,
    factors_hbm,
    dense_ref,
    sib_ref,
    left_ref,
    coords,
    noise,
    order,
    probes,
    right,
    beside,
    even,
    odd,
    counts,
    slots,
    table,
    ask,
    asked,
    give,
    given,
    part,
    parts,
    outer_part,
    outer_parts,
    total,
    totals,
    pairs,
    back,
    backs,
    outer_back,
    outer_backs,
    ready,
    everyone,
    load_sem,
    send_sem,
    recv_sem,
):
    gx, gy = lax.axis_index("gx"), lax.axis_index("gy")
    points = order.shape[1]
    slot = points // inner
    levels = right.shape[0]
    far = levels - 2
    inner_bits = inner.bit_length() - 1
    outer_bits = outer.bit_length() - 1
    share = PROBES // OWNERS
    late = inner - OWNERS
    half = inner_bits * RANK
    owner = gy < OWNERS

    outer_first = levels - outer_bits
    runs = [slice(a * LEAF, (a + 1) * LEAF) for a in range(points // LEAF)]
    pieces = []
    for run in runs:
        pieces.append((probes_hbm.at[:, run], probes.at[:, run]))
        pieces.append((factors_hbm.at[outer_first:, 1, :, run], right.at[outer_first:, :, run]))
    pieces += [
        (order_hbm, order),
        (coords_hbm, coords),
        (noise_hbm, noise),
        (factors_hbm.at[2:outer_first, 1], right.at[2:outer_first]),
        (factors_hbm.at[:2, 1], right.at[:2]),
        (factors_hbm.at[:2, 0], beside),
        (factors_hbm.at[2:, 0], left_ref),
    ]
    early = 2 * len(runs) + 4
    loads = [
        pltpu.make_async_copy(source, target, load_sem.at[i])
        for i, (source, target) in enumerate(pieces)
    ]
    for load in loads[:early]:
        load.start()
    order_load, coords_load, noise_load, inner_load, near_load, beside_load, *rest_loads = loads[
        2 * len(runs) :
    ]

    barrier = pltpu.get_barrier_semaphore()

    @pl.when(owner)
    def _():
        @pl.loop(0, inner - 1)
        def _(step):
            peer = lax.rem(gy + far_first(step, inner), inner)
            pl.semaphore_signal(barrier, inc=1, device_id={"gy": peer})

        @pl.loop(0, outer - 1)
        def _(step):
            peer = lax.rem(gx + far_first(step, outer), outer)
            pl.semaphore_signal(barrier, inc=1, device_id={"gx": peer})

    @pl.when(jnp.logical_not(owner))
    def _():
        pl.semaphore_wait(barrier, OWNERS)

        @pl.loop(0, OWNERS)
        def _(k):
            pl.semaphore_signal(ready, inc=1, device_id={"gy": k})

    def send(step, source, target, axis, peer, arrival=None):
        pltpu.make_async_remote_copy(
            src_ref=source,
            dst_ref=target,
            send_sem=send_sem.at[step],
            recv_sem=recv_sem.at[step if arrival is None else arrival],
            device_id={axis: peer},
        ).start()

    def others(first, last, body):
        @pl.loop(first, last)
        def _(step):
            k = step + 1 - 2 * lax.rem(step, 2)
            pl.when(k != gy)(lambda: body(k))

    def request(arrival):
        def to(k):
            j = lax.rem(k - gy + inner, inner)
            send(0, ask.at[j], asked.at[j], "gy", k, arrival)

        return to

    def give_part(k):
        send(3, outer_part.at[k], outer_parts.at[gy], "gy", k)

    def give_inner_part(k):
        send(2, part.at[k], parts.at[gy], "gy", k)

    def answer(j):
        own_table = [table[r] for r in range(points // TILE)]
        lists = asked[j]
        give[j] = look_up(own_table, lists[0:1], lists[1:2])
        send(1, give.at[j], given.at[j], "gy", lax.rem(gy - j + inner, inner))

    def wait_all(sems, step, ref, first, count):
        whole = ref.at[pl.ds(first, count)]
        pltpu.make_async_copy(whole, whole, sems.at[step]).wait()

    coeff = 0.0
    for a, run in enumerate(runs):
        loads[2 * a].wait()
        loads[2 * a + 1].wait()
        coeff = coeff + dot(
            probes[:, run], right[outer_first:, :, run].reshape(outer_bits * RANK, LEAF), NT
        )
    for k in range(OWNERS):
        outer_part[k] = coeff[k * share : (k + 1) * share]

    @pl.when(jnp.logical_not(owner))
    def _():
        others(0, OWNERS, give_part)

    order_load.wait()
    wanted = order[...]
    source = ((wanted >> (points.bit_length() - 1)) - gy) & (inner - 1)
    local_index = wanted & (points - 1)
    kind = lax.broadcasted_iota(jnp.int32, (inner, TILE), 0)
    chunks = points // TILE
    for k in range(chunks):
        counts[k * inner : (k + 1) * inner, :] = (
            kind == source[:, k * TILE : (k + 1) * TILE]
        ).astype(jnp.bfloat16)
    before = lax.broadcasted_iota(jnp.int32, (TILE, 2 * TILE), 0)
    column = lax.broadcasted_iota(jnp.int32, (TILE, 2 * TILE), 1)
    ones = ((before < column) | (column >= TILE)).astype(jnp.bfloat16)
    ahead = dot(counts[...], ones)
    offset = jnp.zeros((inner, TILE), jnp.float32)
    for k in range(chunks):
        rows = ahead[k * inner : (k + 1) * inner]
        own_source = source[:, k * TILE : (k + 1) * TILE]
        place = jnp.sum(
            jnp.where(kind == own_source, rows[:, :TILE] + offset, 0.0), axis=0, keepdims=True
        )
        slots[:, k * TILE : (k + 1) * TILE] = own_source * slot + place.astype(jnp.int32)
        offset = offset + rows[:, TILE:]

    place = slots[...]
    upper = lax.broadcasted_iota(jnp.int32, (points // LANES, points), 0) == (place >> 7)
    lower = lax.broadcasted_iota(jnp.int32, (LANES, points), 0) == (place & (LANES - 1))
    low_part = (local_index & 63).astype(jnp.float32)
    high_part = (local_index >> 6).astype(jnp.float32)
    marked = jnp.concatenate(
        [jnp.where(upper, low_part, 0.0), jnp.where(upper, high_part, 0.0)], axis=0
    ).astype(jnp.bfloat16)
    lists = dot(marked, lower.astype(jnp.bfloat16), NT)
    lists = (lists[: points // LANES] + 64.0 * lists[points // LANES :]).astype(jnp.int32)
    for j in range(inner):
        ask[j] = lists[2 * j : 2 * j + 2]

    @pl.when(jnp.logical_not(owner))
    def _():
        others(0, OWNERS, request(7))

    inner_load.wait()
    vectors = probes[...]
    coeff = dot(vectors, right[2:outer_first].reshape(inner_bits * RANK, points), NT)
    for k in range(OWNERS):
        part[k] = coeff[k * share : (k + 1) * share]

    @pl.when(jnp.logical_not(owner))
    def _():
        others(0, OWNERS, give_inner_part)

    for load in loads[early:]:
        load.start()

    coords_load.wait()
    noise_load.wait()
    values = jnp.concatenate([coords[...], noise[...]], axis=0)
    vectors_own = [
        jnp.concatenate(
            [values[:, c * LANES : (c + 1) * LANES] for c in (2 * r, 2 * r + 1)], axis=0
        )
        for r in range(points // TILE)
    ]
    for r in range(points // TILE):
        table[r] = vectors_own[r]

    @pl.when(owner)
    def _():
        parts[pl.ds(gy, 1)] = part[pl.ds(gy, 1)]
        outer_parts[pl.ds(gy, 1)] = outer_part[pl.ds(gy, 1)]
        pl.semaphore_wait(barrier, OWNERS - 1 + outer - 1)
        others(0, OWNERS, give_part)
        others(0, OWNERS, request(0))
        pl.semaphore_wait(ready, late)
        others(OWNERS, inner, request(0))

        for teller, first in ((OWNERS - 1, OWNERS), (0, OWNERS + late // 2)):

            @pl.when(gy == teller)
            def _():
                @pl.loop(first, first + late // 2)
                def _(k):
                    pl.semaphore_signal(everyone, inc=1, device_id={"gy": k})

        others(0, OWNERS, give_inner_part)

    given[0] = look_up(vectors_own, ask[0, 0:1], ask[0, 1:2])

    near_load.wait()
    beside_load.wait()
    near = [
        dot(
            vectors[:, a * LEAF : (a + 1) * LEAF],
            right[:2, :, a * LEAF : (a + 1) * LEAF].reshape(2 * RANK, LEAF),
            NT,
        )
        for a in range(points // LEAF)
    ]
    level = lax.broadcasted_iota(jnp.int32, (PROBES, 2 * RANK), 1) < RANK
    for a in range(points // LEAF):
        other = 2 * (1 - a // 2)
        sibling = jnp.where(level, near[a ^ 1], near[other] + near[other + 1])
        dense_ref[:, a * LEAF : (a + 1) * LEAF] = dot(
            sibling.astype(jnp.bfloat16),
            beside[:, :, a * LEAF : (a + 1) * LEAF].reshape(2 * RANK, LEAF),
        )

    @pl.when(owner)
    def _():
        wait_all(recv_sem, 3, outer_parts, 0, inner - 1)
        sums = [outer_parts[e] for e in range(inner)]
        while len(sums) > 1:
            sums = [sums[2 * g] + sums[2 * g + 1] for g in range(len(sums) // 2)]
        total[...] = sums[0]
        totals[pl.ds(gx, 1)] = sums[0][None]

        @pl.loop(0, outer - 1, unroll=True)
        def _(step):
            peer = lax.rem(gx + far_first(step, outer), outer)
            send(4, total, totals.at[gx], "gx", peer)

    @pl.when(owner)
    def _():
        wait_all(recv_sem, 7, asked, 0, late)
        wait_all(recv_sem, 0, asked, 0, OWNERS - 1)

        @pl.loop(0, inner - 1)
        def _(step):
            answer(far_first(step, inner))

    @pl.when(jnp.logical_not(owner))
    def _():
        pl.semaphore_wait(everyone, 1)
        others(OWNERS, inner, request(7))
        wait_all(recv_sem, 0, asked, 0, OWNERS)
        others(0, OWNERS, lambda k: answer(lax.rem(gy - k + inner, inner)))
        wait_all(recv_sem, 7, asked, 0, late - 1)
        others(OWNERS, inner, lambda k: answer(lax.rem(gy - k + inner, inner)))

    @pl.when(owner)
    def _():
        wait_all(recv_sem, 2, parts, 0, inner - 1)
        lane = lax.broadcasted_iota(jnp.int32, (share, half), 1)
        sums = [[parts[e] for e in range(inner)]]
        for step in range(inner_bits - 1):
            last = sums[-1]
            sums.append([last[2 * g] + last[2 * g + 1] for g in range(len(last) // 2)])
        for d in range(inner):
            picked = sums[inner_bits - 1][(d >> (inner_bits - 1)) ^ 1]
            for h in reversed(range(inner_bits - 1)):
                picked = jnp.where(lane < (h + 1) * RANK, sums[h][(d >> h) ^ 1], picked)
            back[d] = picked
        backs[pl.ds(gy, 1)] = back[pl.ds(gy, 1)]
        others(0, inner, lambda k: send(5, back.at[k], backs.at[gy], "gy", k))

    @pl.when(owner)
    def _():
        wait_all(recv_sem, 4, totals, 0, outer - 1)
        width = outer_bits * RANK
        lane = lax.broadcasted_iota(jnp.int32, (share, width), 1)
        base = 0
        sums = [totals[e] for e in range(outer)]
        picked = None
        for h in range(outer_bits):
            for g, value in enumerate(sums):
                pairs[base + g] = value
            group = gx // 2**h
            sibling = pairs[base + group + 1 - 2 * (group % 2)]
            picked = sibling if picked is None else jnp.where(lane < h * RANK, picked, sibling)
            base += len(sums)
            sums = [sums[2 * g] + sums[2 * g + 1] for g in range(len(sums) // 2)]
        outer_back[...] = picked
        outer_backs[pl.ds(gy, 1)] = picked[None]

        others(0, inner, lambda k: send(6, outer_back, outer_backs.at[gy], "gy", k))

    wait_all(recv_sem, 1, given, 1, inner - 1)
    leaf_products(given, slots, probes, even, odd, dense_ref)

    @pl.when(owner)
    def _():
        wait_all(recv_sem, 5, backs, 0, OWNERS - 1)
        wait_all(recv_sem, 6, outer_backs, 0, OWNERS - 1)

    @pl.when(jnp.logical_not(owner))
    def _():
        wait_all(recv_sem, 5, backs, 0, OWNERS)
        wait_all(recv_sem, 6, outer_backs, 0, OWNERS)

    for k in range(OWNERS):
        sib_ref[k * share : (k + 1) * share, :] = jnp.concatenate(
            [backs[k], outer_backs[k]], axis=1
        )

    for load in rest_loads:
        load.wait()
    wait_all(send_sem, 0, ask, 1, inner - 1)
    wait_all(send_sem, 1, give, 1, inner - 1)

    @pl.when(owner)
    def _():
        wait_all(send_sem, 2, part, 0, OWNERS - 1)
        wait_all(send_sem, 3, outer_part, 0, OWNERS - 1)
        wait_all(send_sem, 4, totals, 0, outer - 1)
        wait_all(send_sem, 5, back, 0, inner - 1)
        wait_all(send_sem, 6, outer_parts, 0, inner - 1)

    @pl.when(jnp.logical_not(owner))
    def _():
        wait_all(send_sem, 2, part, 0, OWNERS)
        wait_all(send_sem, 3, outer_part, 0, OWNERS)


def exchange(inner, outer, coords, noise, order, probes, factors):
    points = probes.shape[1]
    levels = factors.shape[0]
    far = levels - 2
    share = PROBES // OWNERS
    inner_bits = inner.bit_length() - 1
    outer_bits = outer.bit_length() - 1
    wide = far * RANK
    f32, bf16, i32 = jnp.float32, jnp.bfloat16, jnp.int32
    hbm = pl.BlockSpec(memory_space=pltpu.HBM)
    leaf_set = (
        pltpu.VMEM((1, LEAF), f32),
        pltpu.VMEM((LEAF, 32), bf16),
        pltpu.VMEM((32, LEAF), bf16),
        pltpu.VMEM((LEAF, LEAF), bf16),
    )
    vmem = pl.BlockSpec(memory_space=pltpu.VMEM)
    return pl.pallas_call(
        functools.partial(exchange_kernel, inner, outer),
        out_shape=(
            jax.ShapeDtypeStruct((PROBES, points), f32),
            jax.ShapeDtypeStruct((PROBES, wide), f32),
            jax.ShapeDtypeStruct((far, RANK, points), bf16),
        ),
        in_specs=[hbm] * 5,
        out_specs=(vmem, vmem, vmem),
        scratch_shapes=[
            pltpu.VMEM((3, points), f32),
            pltpu.VMEM((1, points), f32),
            pltpu.VMEM((1, points), i32),
            pltpu.VMEM((PROBES, points), bf16),
            pltpu.VMEM((levels, RANK, points), bf16),
            pltpu.VMEM((2, RANK, points), bf16),
            leaf_set,
            leaf_set,
            pltpu.VMEM((inner * points // TILE, TILE), bf16),
            pltpu.VMEM((1, points), i32),
            pltpu.VMEM((points // TILE, 8, LANES), f32),
            pltpu.VMEM((inner, 2, LANES), i32),
            pltpu.VMEM((inner, 2, LANES), i32),
            pltpu.VMEM((inner, 8, LANES), f32),
            pltpu.VMEM((inner, 8, LANES), f32),
            pltpu.VMEM((OWNERS, share, inner_bits * RANK), f32),
            pltpu.VMEM((inner, share, inner_bits * RANK), f32),
            pltpu.VMEM((OWNERS, share, outer_bits * RANK), f32),
            pltpu.VMEM((inner, share, outer_bits * RANK), f32),
            pltpu.VMEM((share, outer_bits * RANK), f32),
            pltpu.VMEM((outer, share, outer_bits * RANK), f32),
            pltpu.VMEM((2 * outer, share, outer_bits * RANK), f32),
            pltpu.VMEM((inner, share, inner_bits * RANK), f32),
            pltpu.VMEM((OWNERS, share, inner_bits * RANK), f32),
            pltpu.VMEM((share, outer_bits * RANK), f32),
            pltpu.VMEM((OWNERS, share, outer_bits * RANK), f32),
            pltpu.SemaphoreType.REGULAR,
            pltpu.SemaphoreType.REGULAR,
            pltpu.SemaphoreType.DMA((2 * (points // LEAF) + 7,)),
            pltpu.SemaphoreType.DMA((7,)),
            pltpu.SemaphoreType.DMA((8,)),
        ],
        compiler_params=pltpu.CompilerParams(
            collective_id=0, has_side_effects=True, vmem_limit_bytes=40 * 2**20
        ),
    )(
        *(
            pltpu.with_memory_space_constraint(array, pltpu.HBM)
            for array in (coords, noise.reshape(1, points), order, probes, factors)
        )
    )


def expand_kernel(dense, sib, left, out_hbm, result, sems):
    points = dense.shape[1]
    width = result.shape[2]
    writes = []
    rounded = sib[...].astype(jnp.bfloat16)
    for c in range(points // width):
        columns = slice(c * width, (c + 1) * width)
        result[c] = dense[:, columns] + dot(
            rounded, left[:, :, columns].reshape(sib.shape[1], width)
        )
        writes.append(
            pltpu.make_async_copy(result.at[c], out_hbm.at[:, columns], sems.at[c])
        )
        writes[-1].start()
    for write in writes:
        write.wait()


def expand(dense, sib, left):
    points = dense.shape[1]
    width = 512
    vmem = pl.BlockSpec(memory_space=pltpu.VMEM)
    return pl.pallas_call(
        expand_kernel,
        out_shape=jax.ShapeDtypeStruct((PROBES, points), jnp.float32),
        in_specs=[vmem] * 3,
        out_specs=pl.BlockSpec(memory_space=pltpu.HBM),
        scratch_shapes=[
            pltpu.VMEM((points // width, PROBES, width), jnp.float32),
            pltpu.SemaphoreType.DMA((points // width,)),
        ],
        compiler_params=pltpu.CompilerParams(vmem_limit_bytes=16 * 2**20),
    )(dense, sib, left)


def solution(mesh):
    inner, outer = mesh.shape["gy"], mesh.shape["gx"]

    def local(coords, noise, order, probes, factors):
        return expand(*exchange(inner, outer, coords, noise, order, probes, factors))

    return jax.shard_map(
        local,
        mesh=mesh,
        in_specs=(
            P(None, ("gx", "gy")),
            P(("gx", "gy")),
            P("gx", "gy"),
            P(None, ("gx", "gy")),
            P(None, None, None, ("gx", "gy")),
        ),
        out_specs=P(None, ("gx", "gy")),
        check_vma=False,
    )
```

```python
import functools

import jax
import jax.numpy as jnp
from jax import lax
from jax.experimental import pallas as pl
from jax.experimental.pallas import tpu as pltpu
from jax.sharding import PartitionSpec as P

LEAF = 1024
RANK = 32
PROBES = 64
LANES = 128
TILE = 256
OWNERS = 8
NT = (((1,), (1,)), ((), ()))
SQRT_THREE = 1.7320508075688772
LOG2_E = 1.4426950408889634


def dot(a, b, dims=(((1,), (0,)), ((), ()))):
    return lax.dot_general(a, b, dims, preferred_element_type=jnp.float32)


def look_up(table, first, second):
    shape = (8, LANES)
    found = []
    for picks in (first, second):
        picks = jnp.broadcast_to(picks, shape)
        lane = picks & (LANES - 1)
        out = [
            jnp.take_along_axis(vector, lane, axis=1, mode="promise_in_bounds") for vector in table
        ]
        bit = 8
        while len(out) > 1:
            odd = ((picks >> bit) & 1) == 1
            out = [jnp.where(odd, out[g + 1], out[g]) for g in range(0, len(out), 2)]
            bit += 1
        found.append((out[0], ((picks >> 7) & 1) == 0))
    row = lax.broadcasted_iota(jnp.int32, shape, 0)
    (one, one_low), (two, two_low) = found
    return jnp.where(
        row < 4,
        jnp.where(one_low, one, pltpu.roll(one, 4, 0)),
        jnp.where(two_low, pltpu.roll(two, 4, 0), two),
    )


def split_three(x):
    one = x.astype(jnp.bfloat16)
    rest = x - one.astype(jnp.float32)
    two = rest.astype(jnp.bfloat16)
    three = (rest - two.astype(jnp.float32)).astype(jnp.bfloat16)
    return one.astype(jnp.float32), two.astype(jnp.float32), three.astype(jnp.float32)


def far_first(step, size):
    odd = lax.rem(step, 2)
    return size // 2 + odd * ((step + 1) // 2) - (1 - odd) * (step // 2)


def leaf_features(values):
    spots = (values[0:3] - 4.0) * SQRT_THREE
    norm = spots * spots
    norm = norm[0:1] + norm[1:2] + norm[2:3]
    a, b, c = split_three(spots)
    n1, n2, n3 = split_three(norm)
    unit = jnp.ones_like(norm)
    pad = jnp.zeros((8, norm.shape[1]), jnp.float32)
    one = jnp.concatenate([a, a, b, a, c, b, n1, n2, n3, unit, unit, unit, pad], axis=0)
    two = jnp.concatenate(
        [-2.0 * v for v in (a, b, a, c, a, b)] + [unit, unit, unit, n1, n2, n3, pad], axis=0
    )
    return one.astype(jnp.bfloat16), two.astype(jnp.bfloat16)


def matern(square):
    scaled = square * lax.rsqrt(jnp.maximum(square, 1e-3))
    return (1.0 + scaled) * jnp.exp2(scaled * -LOG2_E)


def leaf_products(given, slots, probes, even, odd, out_ref):
    points = slots.shape[1]
    half = TILE // 2
    tiles = LEAF // TILE

    def multiply(leaf, j, block_ref):
        start = leaf * LEAF
        first, last = j * TILE, (j + 1) * TILE
        columns = slice(start + first, start + last)
        total = out_ref[:, columns] + dot(
            probes[:, start : start + last], block_ref[:last, first:last]
        )
        if j < tiles - 1:
            total = total + dot(
                probes[:, start + last : start + LEAF], block_ref[first:last, last:], NT
            )
        out_ref[:, columns] = total

    def find(leaf, j, noise_ref, one_ref, two_ref, block_ref):
        at = leaf * LEAF + j * TILE
        found = look_up(
            [given[r] for r in range(given.shape[0])],
            slots[:, pl.ds(pl.multiple_of(at, LANES), LANES)],
            slots[:, pl.ds(pl.multiple_of(at + LANES, LANES), LANES)],
        )
        columns = slice(j * TILE, (j + 1) * TILE)
        values = jnp.concatenate([found[0:4], found[4:8]], axis=1)
        one, two = leaf_features(values)
        one_ref[columns, :] = one.T
        two_ref[:, columns] = two
        noise_ref[:, columns] = 1.0 + values[3:4]

    def fill(j, noise_ref, one_ref, two_ref, block_ref):
        first, middle, last = j * TILE, j * TILE + half, (j + 1) * TILE
        eye = lax.broadcasted_iota(jnp.int32, (half, half), 0) == lax.broadcasted_iota(
            jnp.int32, (half, half), 1
        )
        if j:
            block_ref[:first, first:last] = matern(
                dot(one_ref[:first], two_ref[:, first:last])
            ).astype(jnp.bfloat16)
        upper = matern(dot(one_ref[first:middle], two_ref[:, first:last]))
        side = upper[:, half:].astype(jnp.bfloat16)
        block_ref[first:middle, first:middle] = jnp.where(
            eye, noise_ref[:, first:middle], upper[:, :half]
        ).astype(jnp.bfloat16)
        block_ref[first:middle, middle:last] = side
        block_ref[middle:last, first:middle] = side.T
        block_ref[middle:last, middle:last] = jnp.where(
            eye,
            noise_ref[:, middle:last],
            matern(dot(one_ref[middle:last], two_ref[:, middle:last])),
        ).astype(jnp.bfloat16)

    leaves = points // LEAF

    sets = (even, odd)
    for j in range(tiles):
        find(0, j, *even)
    for leaf in range(leaves):
        now, other = sets[leaf % 2], sets[(leaf + 1) % 2]
        for j in range(tiles):
            fill(j, *now)
            if leaf:
                multiply(leaf - 1, j, other[3])
            if leaf + 1 < leaves:
                find(leaf + 1, j, *other)
    for j in range(tiles):
        multiply(leaves - 1, j, sets[(leaves - 1) % 2][3])


def exchange_kernel(
    inner,
    outer,
    coords_hbm,
    noise_hbm,
    order_hbm,
    probes_hbm,
    factors_hbm,
    dense_ref,
    sib_ref,
    left_ref,
    coords,
    noise,
    order,
    probes,
    right,
    beside,
    even,
    odd,
    counts,
    slots,
    table,
    ask,
    asked,
    give,
    given,
    part,
    parts,
    outer_part,
    outer_parts,
    total,
    totals,
    pairs,
    back,
    backs,
    outer_back,
    outer_backs,
    ready,
    everyone,
    load_sem,
    send_sem,
    recv_sem,
):
    gx, gy = lax.axis_index("gx"), lax.axis_index("gy")
    points = order.shape[1]
    slot = points // inner
    levels = right.shape[0]
    far = levels - 2
    inner_bits = inner.bit_length() - 1
    outer_bits = outer.bit_length() - 1
    share = PROBES // OWNERS
    late = inner - OWNERS
    half = inner_bits * RANK
    owner = gy < OWNERS

    outer_first = levels - outer_bits
    runs = [slice(a * LEAF, (a + 1) * LEAF) for a in range(points // LEAF)]
    pieces = []
    for run in runs:
        pieces.append((probes_hbm.at[:, run], probes.at[:, run]))
        pieces.append((factors_hbm.at[outer_first:, 1, :, run], right.at[outer_first:, :, run]))
    pieces += [
        (order_hbm, order),
        (coords_hbm, coords),
        (noise_hbm, noise),
        (factors_hbm.at[2:outer_first, 1], right.at[2:outer_first]),
        (factors_hbm.at[:2, 1], right.at[:2]),
        (factors_hbm.at[:2, 0], beside),
        (factors_hbm.at[2:, 0], left_ref),
    ]
    early = 2 * len(runs) + 4
    loads = [
        pltpu.make_async_copy(source, target, load_sem.at[i])
        for i, (source, target) in enumerate(pieces)
    ]
    for load in loads[:early]:
        load.start()
    order_load, coords_load, noise_load, inner_load, near_load, beside_load, *rest_loads = loads[
        2 * len(runs) :
    ]

    barrier = pltpu.get_barrier_semaphore()

    @pl.when(owner)
    def _():
        @pl.loop(0, inner - 1)
        def _(step):
            peer = lax.rem(gy + far_first(step, inner), inner)
            pl.semaphore_signal(barrier, inc=1, device_id={"gy": peer})

        @pl.loop(0, outer - 1)
        def _(step):
            peer = lax.rem(gx + far_first(step, outer), outer)
            pl.semaphore_signal(barrier, inc=1, device_id={"gx": peer})

    @pl.when(jnp.logical_not(owner))
    def _():
        pl.semaphore_wait(barrier, OWNERS)

        @pl.loop(0, OWNERS)
        def _(k):
            pl.semaphore_signal(ready, inc=1, device_id={"gy": k})

    def send(step, source, target, axis, peer, arrival=None):
        pltpu.make_async_remote_copy(
            src_ref=source,
            dst_ref=target,
            send_sem=send_sem.at[step],
            recv_sem=recv_sem.at[step if arrival is None else arrival],
            device_id={axis: peer},
        ).start()

    def others(first, last, body):
        @pl.loop(first, last)
        def _(step):
            k = step + 1 - 2 * lax.rem(step, 2)
            pl.when(k != gy)(lambda: body(k))

    def request(arrival):
        def to(k):
            j = lax.rem(k - gy + inner, inner)
            send(0, ask.at[j], asked.at[j], "gy", k, arrival)

        return to

    def give_part(k):
        send(3, outer_part.at[k], outer_parts.at[gy], "gy", k)

    def give_inner_part(k):
        send(2, part.at[k], parts.at[gy], "gy", k)

    def answer(j):
        own_table = [table[r] for r in range(points // TILE)]
        lists = asked[j]
        give[j] = look_up(own_table, lists[0:1], lists[1:2])
        send(1, give.at[j], given.at[j], "gy", lax.rem(gy - j + inner, inner))

    def wait_all(sems, step, ref, first, count):
        whole = ref.at[pl.ds(first, count)]
        pltpu.make_async_copy(whole, whole, sems.at[step]).wait()

    coeff = 0.0
    for a, run in enumerate(runs):
        loads[2 * a].wait()
        loads[2 * a + 1].wait()
        coeff = coeff + dot(
            probes[:, run], right[outer_first:, :, run].reshape(outer_bits * RANK, LEAF), NT
        )
    for k in range(OWNERS):
        outer_part[k] = coeff[k * share : (k + 1) * share]

    @pl.when(jnp.logical_not(owner))
    def _():
        for k in range(OWNERS):
            give_part(k)

    order_load.wait()
    wanted = order[...]
    source = ((wanted >> (points.bit_length() - 1)) - gy) & (inner - 1)
    local_index = wanted & (points - 1)
    kind = lax.broadcasted_iota(jnp.int32, (inner, TILE), 0)
    chunks = points // TILE
    for k in range(chunks):
        counts[k * inner : (k + 1) * inner, :] = (
            kind == source[:, k * TILE : (k + 1) * TILE]
        ).astype(jnp.bfloat16)
    before = lax.broadcasted_iota(jnp.int32, (TILE, 2 * TILE), 0)
    column = lax.broadcasted_iota(jnp.int32, (TILE, 2 * TILE), 1)
    ones = ((before < column) | (column >= TILE)).astype(jnp.bfloat16)
    ahead = dot(counts[...], ones)
    offset = jnp.zeros((inner, TILE), jnp.float32)
    for k in range(chunks):
        rows = ahead[k * inner : (k + 1) * inner]
        own_source = source[:, k * TILE : (k + 1) * TILE]
        place = jnp.sum(
            jnp.where(kind == own_source, rows[:, :TILE] + offset, 0.0), axis=0, keepdims=True
        )
        slots[:, k * TILE : (k + 1) * TILE] = own_source * slot + place.astype(jnp.int32)
        offset = offset + rows[:, TILE:]

    place = slots[...]
    upper = lax.broadcasted_iota(jnp.int32, (points // LANES, points), 0) == (place >> 7)
    lower = lax.broadcasted_iota(jnp.int32, (LANES, points), 0) == (place & (LANES - 1))
    low_part = (local_index & 63).astype(jnp.float32)
    high_part = (local_index >> 6).astype(jnp.float32)
    marked = jnp.concatenate(
        [jnp.where(upper, low_part, 0.0), jnp.where(upper, high_part, 0.0)], axis=0
    ).astype(jnp.bfloat16)
    lists = dot(marked, lower.astype(jnp.bfloat16), NT)
    lists = (lists[: points // LANES] + 64.0 * lists[points // LANES :]).astype(jnp.int32)
    for j in range(inner):
        ask[j] = lists[2 * j : 2 * j + 2]

    @pl.when(jnp.logical_not(owner))
    def _():
        others(0, OWNERS, request(7))

    inner_load.wait()
    vectors = probes[...]
    coeff = dot(vectors, right[2:outer_first].reshape(inner_bits * RANK, points), NT)
    for k in range(OWNERS):
        part[k] = coeff[k * share : (k + 1) * share]

    @pl.when(jnp.logical_not(owner))
    def _():
        others(0, OWNERS, give_inner_part)

    for load in loads[early:]:
        load.start()

    coords_load.wait()
    noise_load.wait()
    values = jnp.concatenate([coords[...], noise[...]], axis=0)
    vectors_own = [
        jnp.concatenate(
            [values[:, c * LANES : (c + 1) * LANES] for c in (2 * r, 2 * r + 1)], axis=0
        )
        for r in range(points // TILE)
    ]
    for r in range(points // TILE):
        table[r] = vectors_own[r]

    @pl.when(owner)
    def _():
        parts[pl.ds(gy, 1)] = part[pl.ds(gy, 1)]
        outer_parts[pl.ds(gy, 1)] = outer_part[pl.ds(gy, 1)]
        pl.semaphore_wait(barrier, OWNERS - 1 + outer - 1)
        others(0, OWNERS, give_part)
        others(0, OWNERS, request(0))
        pl.semaphore_wait(ready, late)
        others(OWNERS, inner, request(0))

        for teller, first in ((OWNERS - 1, OWNERS), (0, OWNERS + late // 2)):

            @pl.when(gy == teller)
            def _():
                @pl.loop(first, first + late // 2)
                def _(k):
                    pl.semaphore_signal(everyone, inc=1, device_id={"gy": k})

        others(0, OWNERS, give_inner_part)

    given[0] = look_up(vectors_own, ask[0, 0:1], ask[0, 1:2])

    near_load.wait()
    beside_load.wait()
    near = [
        dot(
            vectors[:, a * LEAF : (a + 1) * LEAF],
            right[:2, :, a * LEAF : (a + 1) * LEAF].reshape(2 * RANK, LEAF),
            NT,
        )
        for a in range(points // LEAF)
    ]
    level = lax.broadcasted_iota(jnp.int32, (PROBES, 2 * RANK), 1) < RANK
    for a in range(points // LEAF):
        other = 2 * (1 - a // 2)
        sibling = jnp.where(level, near[a ^ 1], near[other] + near[other + 1])
        dense_ref[:, a * LEAF : (a + 1) * LEAF] = dot(
            sibling.astype(jnp.bfloat16),
            beside[:, :, a * LEAF : (a + 1) * LEAF].reshape(2 * RANK, LEAF),
        )

    @pl.when(owner)
    def _():
        wait_all(recv_sem, 3, outer_parts, 0, inner - 1)
        sums = [outer_parts[e] for e in range(inner)]
        while len(sums) > 1:
            sums = [sums[2 * g] + sums[2 * g + 1] for g in range(len(sums) // 2)]
        total[...] = sums[0]
        totals[pl.ds(gx, 1)] = sums[0][None]

        @pl.loop(0, outer - 1, unroll=True)
        def _(step):
            peer = lax.rem(gx + far_first(step, outer), outer)
            send(4, total, totals.at[gx], "gx", peer)

    @pl.when(owner)
    def _():
        wait_all(recv_sem, 7, asked, 0, late)
        wait_all(recv_sem, 0, asked, 0, OWNERS - 1)

        @pl.loop(0, inner - 1)
        def _(step):
            answer(far_first(step, inner))

    @pl.when(jnp.logical_not(owner))
    def _():
        pl.semaphore_wait(everyone, 1)
        others(OWNERS, inner, request(7))
        wait_all(recv_sem, 0, asked, 0, OWNERS)
        others(0, OWNERS, lambda k: answer(lax.rem(gy - k + inner, inner)))
        wait_all(recv_sem, 7, asked, 0, late - 1)
        others(OWNERS, inner, lambda k: answer(lax.rem(gy - k + inner, inner)))

    @pl.when(owner)
    def _():
        wait_all(recv_sem, 2, parts, 0, inner - 1)
        lane = lax.broadcasted_iota(jnp.int32, (share, half), 1)
        sums = [[parts[e] for e in range(inner)]]
        for step in range(inner_bits - 1):
            last = sums[-1]
            sums.append([last[2 * g] + last[2 * g + 1] for g in range(len(last) // 2)])
        for d in range(inner):
            picked = sums[inner_bits - 1][(d >> (inner_bits - 1)) ^ 1]
            for h in reversed(range(inner_bits - 1)):
                picked = jnp.where(lane < (h + 1) * RANK, sums[h][(d >> h) ^ 1], picked)
            back[d] = picked.astype(jnp.bfloat16)
        backs[pl.ds(gy, 1)] = back[pl.ds(gy, 1)]
        others(0, inner, lambda k: send(5, back.at[k], backs.at[gy], "gy", k))

    @pl.when(owner)
    def _():
        wait_all(recv_sem, 4, totals, 0, outer - 1)
        width = outer_bits * RANK
        lane = lax.broadcasted_iota(jnp.int32, (share, width), 1)
        base = 0
        sums = [totals[e] for e in range(outer)]
        picked = None
        for h in range(outer_bits):
            for g, value in enumerate(sums):
                pairs[base + g] = value
            group = gx // 2**h
            sibling = pairs[base + group + 1 - 2 * (group % 2)]
            picked = sibling if picked is None else jnp.where(lane < h * RANK, picked, sibling)
            base += len(sums)
            sums = [sums[2 * g] + sums[2 * g + 1] for g in range(len(sums) // 2)]
        rounded = picked.astype(jnp.bfloat16)[None]
        outer_back[...] = rounded
        outer_backs[pl.ds(gy, 1)] = rounded


        @pl.loop(1, inner, unroll=True)
        def _(j):
            send(6, outer_back.at[0], outer_backs.at[gy], "gy", lax.rem(gy - j + inner, inner))

    wait_all(recv_sem, 1, given, 1, inner - 1)
    leaf_products(given, slots, probes, even, odd, dense_ref)

    @pl.when(owner)
    def _():
        wait_all(recv_sem, 5, backs, 0, OWNERS - 1)
        wait_all(recv_sem, 6, outer_backs, 0, OWNERS - 1)

    @pl.when(jnp.logical_not(owner))
    def _():
        wait_all(recv_sem, 5, backs, 0, OWNERS)
        wait_all(recv_sem, 6, outer_backs, 0, OWNERS)

    for k in range(OWNERS):
        sib_ref[k * share : (k + 1) * share, :] = jnp.concatenate(
            [backs[k], outer_backs[k]], axis=1
        ).astype(jnp.float32)

    for load in rest_loads:
        load.wait()
    wait_all(send_sem, 0, ask, 1, inner - 1)
    wait_all(send_sem, 1, give, 1, inner - 1)

    @pl.when(owner)
    def _():
        wait_all(send_sem, 2, part, 0, OWNERS - 1)
        wait_all(send_sem, 3, outer_part, 0, OWNERS - 1)
        wait_all(send_sem, 4, totals, 0, outer - 1)
        wait_all(send_sem, 5, back, 0, inner - 1)
        wait_all(send_sem, 6, back, 0, inner - 1)

    @pl.when(jnp.logical_not(owner))
    def _():
        wait_all(send_sem, 2, part, 0, OWNERS)
        wait_all(send_sem, 3, outer_part, 0, OWNERS)


def exchange(inner, outer, coords, noise, order, probes, factors):
    points = probes.shape[1]
    levels = factors.shape[0]
    far = levels - 2
    share = PROBES // OWNERS
    inner_bits = inner.bit_length() - 1
    outer_bits = outer.bit_length() - 1
    wide = far * RANK
    f32, bf16, i32 = jnp.float32, jnp.bfloat16, jnp.int32
    hbm = pl.BlockSpec(memory_space=pltpu.HBM)
    leaf_set = (
        pltpu.VMEM((1, LEAF), f32),
        pltpu.VMEM((LEAF, 32), bf16),
        pltpu.VMEM((32, LEAF), bf16),
        pltpu.VMEM((LEAF, LEAF), bf16),
    )
    vmem = pl.BlockSpec(memory_space=pltpu.VMEM)
    return pl.pallas_call(
        functools.partial(exchange_kernel, inner, outer),
        out_shape=(
            jax.ShapeDtypeStruct((PROBES, points), f32),
            jax.ShapeDtypeStruct((PROBES, wide), f32),
            jax.ShapeDtypeStruct((far, RANK, points), bf16),
        ),
        in_specs=[hbm] * 5,
        out_specs=(vmem, vmem, vmem),
        scratch_shapes=[
            pltpu.VMEM((3, points), f32),
            pltpu.VMEM((1, points), f32),
            pltpu.VMEM((1, points), i32),
            pltpu.VMEM((PROBES, points), bf16),
            pltpu.VMEM((levels, RANK, points), bf16),
            pltpu.VMEM((2, RANK, points), bf16),
            leaf_set,
            leaf_set,
            pltpu.VMEM((inner * points // TILE, TILE), bf16),
            pltpu.VMEM((1, points), i32),
            pltpu.VMEM((points // TILE, 8, LANES), f32),
            pltpu.VMEM((inner, 2, LANES), i32),
            pltpu.VMEM((inner, 2, LANES), i32),
            pltpu.VMEM((inner, 8, LANES), f32),
            pltpu.VMEM((inner, 8, LANES), f32),
            pltpu.VMEM((OWNERS, share, inner_bits * RANK), f32),
            pltpu.VMEM((inner, share, inner_bits * RANK), f32),
            pltpu.VMEM((OWNERS, share, outer_bits * RANK), f32),
            pltpu.VMEM((inner, share, outer_bits * RANK), f32),
            pltpu.VMEM((share, outer_bits * RANK), f32),
            pltpu.VMEM((outer, share, outer_bits * RANK), f32),
            pltpu.VMEM((2 * outer, share, outer_bits * RANK), f32),
            pltpu.VMEM((inner, share, inner_bits * RANK), bf16),
            pltpu.VMEM((OWNERS, share, inner_bits * RANK), bf16),
            pltpu.VMEM((1, share, outer_bits * RANK), bf16),
            pltpu.VMEM((OWNERS, share, outer_bits * RANK), bf16),
            pltpu.SemaphoreType.REGULAR,
            pltpu.SemaphoreType.REGULAR,
            pltpu.SemaphoreType.DMA((2 * (points // LEAF) + 7,)),
            pltpu.SemaphoreType.DMA((7,)),
            pltpu.SemaphoreType.DMA((8,)),
        ],
        compiler_params=pltpu.CompilerParams(
            collective_id=0, has_side_effects=True, vmem_limit_bytes=40 * 2**20
        ),
    )(
        *(
            pltpu.with_memory_space_constraint(array, pltpu.HBM)
            for array in (coords, noise.reshape(1, points), order, probes, factors)
        )
    )


def expand_kernel(dense, sib, left, out_hbm, result, sems):
    points = dense.shape[1]
    width = result.shape[2]
    writes = []
    rounded = sib[...].astype(jnp.bfloat16)
    for c in range(points // width):
        columns = slice(c * width, (c + 1) * width)
        result[c] = dense[:, columns] + dot(
            rounded, left[:, :, columns].reshape(sib.shape[1], width)
        )
        writes.append(
            pltpu.make_async_copy(result.at[c], out_hbm.at[:, columns], sems.at[c])
        )
        writes[-1].start()
    for write in writes:
        write.wait()


def expand(dense, sib, left):
    points = dense.shape[1]
    width = 512
    vmem = pl.BlockSpec(memory_space=pltpu.VMEM)
    return pl.pallas_call(
        expand_kernel,
        out_shape=jax.ShapeDtypeStruct((PROBES, points), jnp.float32),
        in_specs=[vmem] * 3,
        out_specs=pl.BlockSpec(memory_space=pltpu.HBM),
        scratch_shapes=[
            pltpu.VMEM((points // width, PROBES, width), jnp.float32),
            pltpu.SemaphoreType.DMA((points // width,)),
        ],
        compiler_params=pltpu.CompilerParams(vmem_limit_bytes=16 * 2**20),
    )(dense, sib, left)


def solution(mesh):
    inner, outer = mesh.shape["gy"], mesh.shape["gx"]

    def local(coords, noise, order, probes, factors):
        return expand(*exchange(inner, outer, coords, noise, order, probes, factors))

    return jax.shard_map(
        local,
        mesh=mesh,
        in_specs=(
            P(None, ("gx", "gy")),
            P(("gx", "gy")),
            P("gx", "gy"),
            P(None, ("gx", "gy")),
            P(None, None, None, ("gx", "gy")),
        ),
        out_specs=P(None, ("gx", "gy")),
        check_vma=False,
    )
```
